32 devices in a mesh: ta: 4 (over z), ha: 4 (over x, core), wa: 2 (over y).
Axes of the slice: x: 2, y: 2, z: 4, core: 2. Of those that a mesh axis runs over, the one named last changes fastest.
Arguments:
- features: bfloat16 [16, 64, 32, 256], P('ta', 'ha', 'wa'), may hold values from -6 to 6
- norm_gain: float32 [256], replicated, may hold values from 0.5 to 1.5
- conv_weight: bfloat16 [3, 3, 3, 256, 256], replicated, may hold values from -0.078125 to 0.078125
- cotangent: bfloat16 [16, 64, 32, 256], P('ta', 'ha', 'wa'), may hold values from -6 to 6
Outputs:
- decoded: bfloat16 [16, 64, 32, 256], P('ta', 'ha', 'wa')
- grad_features: bfloat16 [16, 64, 32, 256], P('ta', 'ha', 'wa')
- grad_weight: float32 [3, 3, 3, 256, 256], P(None, None, None, None, ('ha', 'wa'))
The draws below stay inside these ranges and needn't reach their ends.
All inputs are finite; a program needn't handle non-finite values.
Results may differ from the reference program's by a relative error of at most 0.0032.
Values may be sent and summed in bfloat16 or wider, within the bound.
No kernel may reach another device: no remote copies, remote signals or barrier semaphores. Data moves between devices by JAX's collectives and lax.ppermute only.
A program may use at most 128 MiB of HBM per device.

```python
import jax
import jax.numpy as jnp
from jax import lax

C = 256
FRAMES = 16
HEIGHT = 64
WIDTH = 32
VOXELS = 32768


def levels(rng, shape, cuts, low, high):
    factor_of, own = 1.0, jax.random.fold_in(rng, 6)
    for axis_at, blocks in cuts:
        draws = jnp.exp(jax.random.uniform(jax.random.fold_in(own, axis_at), (blocks,), jnp.float32, low / len(cuts), high / len(cuts)))
        factor_of = factor_of * jnp.repeat(draws, shape[axis_at] // blocks).reshape([-1 if axis == axis_at else 1 for axis in range(len(shape))])
    return factor_of


def normal_values(rng, shape, spread, reach, pieces=(), dtype=jnp.bfloat16):
    level = levels(rng, shape, pieces, -0.22, 0.18) if pieces else 1.0
    drawn = jax.random.normal(rng, shape, jnp.float32) * spread * level
    return jnp.minimum(jnp.maximum(drawn, -reach), reach).astype(dtype)


def setup_inputs(seed: int = 0) -> dict:
    streams_of = jax.random.split(jax.random.key(seed), 5)
    features = normal_values(streams_of[0], (FRAMES, HEIGHT, WIDTH, C), 1.0, 6.0, ((0, 4), (1, 4), (2, 2)))
    norm_gain = jnp.clip(jax.random.uniform(streams_of[1], (C,), jnp.float32, 0.5, 1.5), 0.5, 1.5)
    conv_weight = normal_values(streams_of[2], (3, 3, 3, C, C), (27 * C) ** -0.5, 0.078125)
    cotangent = normal_values(streams_of[3], (FRAMES, HEIGHT, WIDTH, C), 1.0, 6.0, ((0, 4), (1, 4), (2, 2)))
    return dict(features=features, norm_gain=norm_gain, conv_weight=conv_weight, cotangent=cotangent)


EPSILON = 1e-06

def activate(features, norm_gain):
    values = features.astype(jnp.float32)
    inverse = lax.rsqrt(lax.optimization_barrier(jnp.mean(values * values, axis=-1, keepdims=True)) + EPSILON)
    unit_rms = values * inverse
    normed = unit_rms * norm_gain
    activated = (normed * jax.nn.sigmoid(normed)).astype(jnp.bfloat16)
    return (values, inverse, unit_rms, normed, activated)

def norm_backward(grad_act, normed, unit_rms, inverse, norm_gain):
    logistic = jax.nn.sigmoid(normed)
    grad_normed = grad_act * logistic * (1.0 + normed * (1.0 - logistic))
    grad_unit = grad_normed * norm_gain
    return inverse * (grad_unit - unit_rms * lax.optimization_barrier(jnp.mean(grad_unit * unit_rms, axis=-1, keepdims=True)))

def reference(features, norm_gain, conv_weight, cotangent):
    frames, height, width, channels = features.shape
    values, inverse, unit_rms, normed, activated = activate(features, norm_gain)
    padded = jnp.pad(activated, ((2, 0), (1, 1), (1, 1), (0, 0))).astype(jnp.float32)
    kernel = conv_weight.astype(jnp.float32)
    grad_out = cotangent.astype(jnp.float32)
    flat_grad = grad_out.reshape(-1, channels)
    grad_padded = jnp.pad(grad_out, ((0, 2), (1, 1), (1, 1), (0, 0)))
    mixed = jnp.zeros((frames * height * width, channels), jnp.float32)
    grad_act = jnp.zeros((frames * height * width, channels), jnp.float32)
    weight_taps = []
    for t_off in range(3):
        for h_off in range(3):
            for w_off in range(3):
                window = padded[t_off:t_off + frames, h_off:h_off + height, w_off:w_off + width].reshape(-1, channels)
                mixed = mixed + jnp.dot(window, kernel[t_off, h_off, w_off], precision=lax.Precision.HIGHEST)
                weight_taps.append(lax.dot_general(window, flat_grad, (((0,), (0,)), ((), ())), precision=lax.Precision.HIGHEST))
                back = grad_padded[2 - t_off:2 - t_off + frames, 2 - h_off:2 - h_off + height, 2 - w_off:2 - w_off + width].reshape(-1, channels)
                grad_act = grad_act + jnp.dot(back, kernel[t_off, h_off, w_off].T, precision=lax.Precision.HIGHEST)
    grad_weight = jnp.stack(weight_taps).reshape(3, 3, 3, channels, channels) * VOXELS ** (-0.5)
    decoded = (values + mixed.reshape(features.shape)).astype(jnp.bfloat16)
    grad_norm = norm_backward(grad_act.reshape(features.shape), normed, unit_rms, inverse, norm_gain)
    grad_features = (grad_out + grad_norm).astype(jnp.bfloat16)
    return (decoded, grad_features, grad_weight)
```

```python
import functools

import jax
import jax.numpy as jnp
from jax import lax
from jax.experimental import pallas as pl
from jax.experimental.pallas import tpu as pltpu
from jax.sharding import PartitionSpec as P

EPSILON = 1e-06
AXES = ("ta", "ha", "wa")
BF16 = jnp.bfloat16
F32 = jnp.float32
VMEM_LIMIT = 48 * 1024 * 1024


def dot(a, b):
    return jnp.dot(a, b, preferred_element_type=F32)


def dot_t(a, b):
    return lax.dot_general(a, b, (((1,), (1,)), ((), ())), preferred_element_type=F32)


def call(kernel, out_shape, flops, moved, scratch=()):
    return pl.pallas_call(
        kernel,
        out_shape=out_shape,
        scratch_shapes=list(scratch),
        compiler_params=pltpu.CompilerParams(vmem_limit_bytes=VMEM_LIMIT),
        cost_estimate=pl.CostEstimate(flops=flops, bytes_accessed=moved, transcendentals=0),
    )


def shift_line(array, axis, by):
    length = lax.axis_size(axis)
    pairs = [(i, i + by) for i in range(length) if 0 <= i + by < length]
    return lax.ppermute(array, axis, pairs)


def swap_core(array):
    length = lax.axis_size("ha")
    return lax.ppermute(array, "ha", [(i, i ^ 1) for i in range(length)])


def to_chip(array, du, dw):
    chips, width = lax.axis_size("ha") // 2, lax.axis_size("wa")
    pairs = []
    for u in range(chips):
        for core in range(2):
            for w in range(width):
                source = (2 * u + core) * width + w
                target = (2 * ((u + du) % chips) + core) * width + (w + dw) % width
                pairs.append((source, target))
    return lax.ppermute(array, ("ha", "wa"), pairs)


def ring(array, axis, by):
    length = lax.axis_size(axis)
    return lax.ppermute(array, axis, [(i, (i + by) % length) for i in range(length)])


def plane_halo(cells):
    for axis, dim in (("wa", 2), ("ha", 1)):
        size = cells.shape[dim]
        head = lax.slice_in_dim(cells, 0, 1, axis=dim)
        tail = lax.slice_in_dim(cells, size - 1, size, axis=dim)
        cells = jnp.concatenate(
            [shift_line(tail, axis, 1), cells, shift_line(head, axis, -1)], axis=dim
        )
    return cells


def activate_kernel(x_ref, gain_ref, act_ref, act_t_ref):
    values = x_ref[...].astype(F32)
    inverse = lax.rsqrt(jnp.mean(values * values, axis=-1, keepdims=True) + EPSILON)
    normed = values * inverse * gain_ref[...]
    activated = (normed * jax.nn.sigmoid(normed)).astype(BF16)
    act_ref[...] = activated
    act_t_ref[...] = activated.T


def spread_columns(source, width, target):
    frames, high, _, channels = source.shape
    for k in range(3):
        target[k] = source[:, :, k : k + width, :].reshape(frames * high * width, channels)


def taps_kernel(height, width, act_a, act_b, cot_a, cot_b, out, spread_a, spread_b):
    frames = cot_a.shape[0]
    spread_columns(cot_a, width, spread_a)
    spread_columns(cot_b, width, spread_b)
    acts = jnp.concatenate([act_a[...], act_b[...]], axis=1)
    part = out.shape[1]

    def shifted(tap):
        j, k = divmod(tap, 3)
        pieces = []
        for spread in (spread_a, spread_b):
            for t in range(frames):
                start = (t * (height + 2) + 2 - j) * width
                pieces.append(spread[2 - k, start : start + height * width, :])
        return jnp.concatenate(pieces, axis=0)

    for first in range(0, 9, 2):
        taps = range(first, min(first + 2, 9))
        terms = dot(acts, jnp.concatenate([shifted(tap) for tap in taps], axis=1)).T
        for place, tap in enumerate(taps):
            out[tap] = terms[place * part : (place + 1) * part].astype(BF16)


def conv_sum(height, width, frames, spread, weight, backward):
    total = None
    for i in range(3):
        for j in range(3):
            at_t, at_h = (2 - i, 2 - j) if backward else (i, j)
            columns = []
            for k in range(3):
                at_w = 2 - k if backward else k
                pieces = []
                for t in range(frames):
                    start = ((t + at_t) * (height + 2) + at_h) * width
                    pieces.append(spread[at_w, start : start + height * width, :])
                columns.append(jnp.concatenate(pieces, axis=0))
            left = jnp.concatenate(columns, axis=1)
            if backward:
                term = dot_t(left, jnp.concatenate([weight[i, j, k] for k in range(3)], axis=1))
            else:
                term = dot(left, jnp.concatenate([weight[i, j, k] for k in range(3)], axis=0))
            total = term if total is None else total + term
    return total


def forward_kernel(height, width, x_ref, padded, weight, out, spread):
    frames = padded.shape[0] - 2
    spread_columns(padded, width, spread)
    mixed = conv_sum(height, width, frames, spread, weight, False)
    out[...] = (x_ref[...].astype(F32) + mixed).astype(BF16)


def backward_kernel(height, width, x_ref, gain_ref, cot_ref, padded, weight, out, spread):
    frames = padded.shape[0] - 2
    spread_columns(padded, width, spread)
    grad_act = conv_sum(height, width, frames, spread, weight, True)
    values = x_ref[...].astype(F32)
    inverse = lax.rsqrt(jnp.mean(values * values, axis=-1, keepdims=True) + EPSILON)
    unit_rms = values * inverse
    gain = gain_ref[...]
    normed = unit_rms * gain
    logistic = jax.nn.sigmoid(normed)
    grad_unit = grad_act * logistic * (1.0 + normed * (1.0 - logistic)) * gain
    grad_norm = inverse * (
        grad_unit - unit_rms * jnp.mean(grad_unit * unit_rms, axis=-1, keepdims=True)
    )
    out[...] = (cot_ref[...].astype(F32) + grad_norm).astype(BF16)


def body(features, norm_gain, conv_weight, cotangent):
    frames, height, width, channels = features.shape
    cells = frames * height * width
    depth, rows_of, cols_of = (lax.axis_size(axis) for axis in AXES)
    chips = rows_of // 2
    owners = rows_of * cols_of
    owned = channels // owners
    half = channels // 2
    me_t, me_h, me_w = (lax.axis_index(axis) for axis in AXES)
    core, chip = me_h % 2, me_h // 2
    flat_x = features.reshape(cells, channels)
    flat_cot = cotangent.reshape(cells, channels)
    gain = norm_gain.reshape(1, channels)
    product = 2 * cells * channels * channels

    act, act_t = call(
        activate_kernel,
        (
            jax.ShapeDtypeStruct((cells, channels), BF16),
            jax.ShapeDtypeStruct((channels, cells), BF16),
        ),
        10 * cells * channels,
        6 * cells * channels,
    )(flat_x, gain)
    act_t_other = swap_core(act_t)

    cot_plane = plane_halo(cotangent)
    cot_later = shift_line(cot_plane[:2], "ta", -1)
    grad_padded = jnp.concatenate([cot_plane, cot_later], axis=0)
    by_core = grad_padded.reshape(grad_padded.shape[:3] + (chips, 2, cols_of * owned))

    def half_of(which):
        first = by_core[..., 0, :].reshape(grad_padded.shape[:3] + (half,))
        second = by_core[..., 1, :].reshape(grad_padded.shape[:3] + (half,))
        return jnp.where(which == 0, first, second)

    mine = half_of(core)
    others = swap_core(half_of(1 - core))

    spread = pltpu.VMEM((3, frames * (height + 2) * width, half), BF16)
    taps = [
        call(
            functools.partial(taps_kernel, height, width),
            jax.ShapeDtypeStruct((9, half, channels), BF16),
            9 * product,
            4 * cells * channels,
            (spread, spread),
        )(act_t, act_t_other, mine[2 - i : 2 - i + frames], others[2 - i : 2 - i + frames])
        for i in range(3)
    ]
    parts = jnp.stack(taps).reshape(27, chips * cols_of, owned, channels)

    def slice_for(du, dw):
        place = ((chip + du) % chips) * cols_of + (me_w + dw) % cols_of
        return lax.dynamic_index_in_dim(parts, place, axis=1, keepdims=False)

    total = slice_for(0, 0).astype(F32)
    for du in range(chips):
        for dw in range(cols_of):
            if du or dw:
                total = total + to_chip(slice_for(du, dw), du, dw).astype(F32)

    total = total.reshape(depth, -1, channels)
    rounded = total.astype(BF16)

    def part_of(array, place):
        return lax.dynamic_index_in_dim(array, place, axis=0, keepdims=False)

    piece = part_of(total, me_t)
    for by in range(1, depth):
        piece = piece + ring(part_of(rounded, (me_t + by) % depth), "ta", by).astype(F32)
    voxels_all = cells * depth * rows_of * cols_of
    piece = (piece * float(voxels_all) ** (-0.5)).astype(BF16)
    pieces = [piece] + [ring(piece, "ta", by) for by in range(1, depth)]
    stacked = jnp.stack(pieces[::-1])
    stacked = jnp.roll(stacked, me_t + 1, axis=0)
    grad_weight = jnp.swapaxes(stacked.reshape(27, owned, channels), 1, 2).astype(F32)
    grad_weight = grad_weight.reshape(3, 3, 3, channels, owned)

    act_plane = plane_halo(act.reshape(features.shape))
    act_earlier = shift_line(act_plane[frames - 2 :], "ta", 1)
    padded = jnp.concatenate([act_earlier, act_plane], axis=0)

    flat = jax.ShapeDtypeStruct((cells, channels), BF16)
    spread = pltpu.VMEM((3, (frames + 2) * (height + 2) * width, channels), BF16)
    moved = conv_weight.size * 2 + 8 * cells * channels
    decoded = call(
        functools.partial(forward_kernel, height, width), flat, 27 * product, moved, (spread,)
    )(flat_x, padded, conv_weight)
    grad_features = call(
        functools.partial(backward_kernel, height, width), flat, 27 * product, moved, (spread,)
    )(flat_x, gain, flat_cot, grad_padded, conv_weight)
    return (
        decoded.reshape(features.shape),
        grad_features.reshape(features.shape),
        grad_weight,
    )


def solution(mesh):
    placed = (P("ta", "ha", "wa", None), P(), P(), P("ta", "ha", "wa", None))
    return jax.shard_map(
        body,
        mesh=mesh,
        in_specs=placed,
        out_specs=(
            P("ta", "ha", "wa", None),
            P("ta", "ha", "wa", None),
            P(None, None, None, None, ("ha", "wa")),
        ),
        check_vma=False,
    )
```

```python
import functools

import jax
import jax.numpy as jnp
from jax import lax
from jax.experimental import pallas as pl
from jax.experimental.pallas import tpu as pltpu
from jax.sharding import PartitionSpec as P

EPSILON = 1e-06
AXES = ("ta", "ha", "wa")
BF16 = jnp.bfloat16
F32 = jnp.float32
VMEM_LIMIT = 48 * 1024 * 1024


def dot(a, b):
    return jnp.dot(a, b, preferred_element_type=F32)


def dot_t(a, b):
    return lax.dot_general(a, b, (((1,), (1,)), ((), ())), preferred_element_type=F32)


def call(kernel, out_shape, flops, moved, scratch=(), scalars=0, arrays=0):
    specs = [pl.BlockSpec(memory_space=pltpu.SMEM)] * scalars
    specs += [pl.BlockSpec(memory_space=pltpu.VMEM)] * arrays
    return pl.pallas_call(
        kernel,
        out_shape=out_shape,
        in_specs=specs,
        scratch_shapes=list(scratch),
        compiler_params=pltpu.CompilerParams(vmem_limit_bytes=VMEM_LIMIT),
        cost_estimate=pl.CostEstimate(flops=flops, bytes_accessed=moved, transcendentals=0),
    )


def shift_line(array, axis, by):
    length = lax.axis_size(axis)
    pairs = [(i, i + by) for i in range(length) if 0 <= i + by < length]
    return lax.ppermute(array, axis, pairs)


def swap_core(array):
    length = lax.axis_size("ha")
    return lax.ppermute(array, "ha", [(i, i ^ 1) for i in range(length)])


def to_chip(array, du, dw):
    chips, width = lax.axis_size("ha") // 2, lax.axis_size("wa")
    pairs = []
    for u in range(chips):
        for core in range(2):
            for w in range(width):
                source = (2 * u + core) * width + w
                target = (2 * ((u + du) % chips) + core) * width + (w + dw) % width
                pairs.append((source, target))
    return lax.ppermute(array, ("ha", "wa"), pairs)


def ring(array, axis, by):
    length = lax.axis_size(axis)
    return lax.ppermute(array, axis, [(i, (i + by) % length) for i in range(length)])


CORNERS = 16


def prepare_kernel(x_ref, cot_ref, gain_ref, act_ref, act_t_ref, up_ref, down_ref, lefts, rights):
    frames, height, width, channels = x_ref.shape
    values = x_ref[...].reshape(-1, channels).astype(F32)
    inverse = lax.rsqrt(jnp.mean(values * values, axis=-1, keepdims=True) + EPSILON)
    normed = values * inverse * gain_ref[...]
    activated = (normed * jax.nn.sigmoid(normed)).astype(BF16)
    act_ref[...] = activated.reshape(x_ref.shape)
    act_t_ref[...] = activated.T
    for place, source in enumerate((cot_ref, act_ref)):
        up_ref[place] = source[:, 0]
        down_ref[place] = source[:, height - 1]
        cells = source[...].astype(F32)
        lefts[place] = cells[:, :, 0, :].astype(BF16)
        rights[place] = cells[:, :, width - 1, :].astype(BF16)


def columns_kernel(lefts, rights, above, below, to_left, to_right):
    _, frames, _, channels = lefts.shape
    width = above.shape[2]
    nothing = jnp.zeros((2, frames, CORNERS - 2, channels), F32)
    for source, target, at in ((lefts, to_left, 0), (rights, to_right, width - 1)):
        over = above[...].astype(F32)[:, :, at : at + 1, :]
        under = below[...].astype(F32)[:, :, at : at + 1, :]
        parts = [source[...].astype(F32), over, under, nothing]
        target[...] = jnp.concatenate(parts, axis=2).astype(BF16)


def halves(core, values, chips):
    block = values.shape[-1] // (2 * chips)
    values = values.astype(F32)
    first, second = (
        jnp.concatenate(
            [
                values[..., (2 * u + which) * block : (2 * u + which + 1) * block]
                for u in range(chips)
            ],
            axis=-1,
        )
        for which in range(2)
    )
    own = jnp.where(core == 0, first, second)
    other = jnp.where(core == 0, second, first)
    return own.astype(BF16), other.astype(BF16)


def bundle_kernel(chips, core_ref, cot, above, below, left, right, cot_edges, act_edges, mine, send):
    core = core_ref[0]
    inner = cot.shape[1]
    for place, target in enumerate((cot_edges, act_edges)):
        target[...] = jnp.concatenate(
            [ref[place] for ref in (above, below, left, right)], axis=1
        )
    mine[:, :inner], send[:, :inner] = halves(core, cot[...], chips)
    mine[:, inner:], send[:, inner:] = halves(core, cot_edges[...], chips)


def later_kernel(chips, core_ref, cot, cot_edges, mine, send):
    core = core_ref[0]
    inner = cot.shape[1]
    mine[:, :inner], send[:, :inner] = halves(core, cot[...], chips)
    mine[:, inner:], send[:, inner:] = halves(core, cot_edges[...], chips)


def spread_frame(center, edges, height, width, target, at):
    channels = center.shape[-1]
    tall = height + CORNERS
    above, below = edges[:width], edges[width : 2 * width]
    rows = jnp.concatenate([above, center, below], axis=0)
    target[1, at : at + (height + 2) * width, :] = rows
    rows = rows.astype(F32).reshape(height + 2, width, channels)
    place = lax.broadcasted_iota(jnp.int32, rows.shape, 1)
    for k, start, edge, by in ((0, 2 * width, 0, 1), (2, 2 * width + tall, width - 1, width - 1)):
        column = edges[start : start + tall].astype(F32)
        column = jnp.concatenate(
            [column[height : height + 1], column[:height], column[height + 1 : height + 2]], axis=0
        )
        moved = jnp.where(place == edge, column[:, None, :], pltpu.roll(rows, by, 1))
        target[k, at : at + (height + 2) * width, :] = moved.astype(BF16).reshape(-1, channels)


def taps_kernel(height, width, offset, frames, *refs):
    places, act_a, act_b, *rest = refs
    count = places.shape[0]
    terms_ref, spread_a, spread_b = rest[-3:]
    outs = rest[-3 - count : -3]
    bundles = rest[: -3 - count]
    inner = height * width
    spreads = (spread_a, spread_b)
    step = (height + 2) * width
    for side, spread in enumerate(spreads):
        for t in range(frames):
            at = t + 2 - offset
            ref = bundles[side] if at < frames else bundles[2 + side]
            frame = ref[at % frames]
            spread_frame(frame[:inner], frame[inner:], height, width, spread, t * step)
    acts = jnp.concatenate([act_a[...], act_b[...]], axis=1)
    part = terms_ref.shape[1]

    def shifted(tap):
        j, k = divmod(tap, 3)
        pieces = []
        for spread in spreads:
            for t in range(frames):
                start = t * step + (2 - j) * width
                pieces.append(spread[2 - k, start : start + inner, :])
        return jnp.concatenate(pieces, axis=0)

    for first in range(0, 9, 2):
        taps = range(first, min(first + 2, 9))
        terms = dot(acts, jnp.concatenate([shifted(tap) for tap in taps], axis=1)).T
        for place, tap in enumerate(taps):
            terms_ref[tap] = terms[place * part : (place + 1) * part]
    owned = part // count
    for place, out in enumerate(outs):
        start = pl.multiple_of(places[place] * owned, owned)
        out[...] = terms_ref[:, pl.ds(start, owned), :].astype(out.dtype)


def conv_sum(height, width, frames, spread, weight, backward):
    total = None
    for i in range(3):
        for j in range(3):
            at_t, at_h = (2 - i, 2 - j) if backward else (i, j)
            columns = []
            for k in range(3):
                at_w = 2 - k if backward else k
                pieces = []
                for t in range(frames):
                    start = ((t + at_t) * (height + 2) + at_h) * width
                    pieces.append(spread[at_w, start : start + height * width, :])
                columns.append(jnp.concatenate(pieces, axis=0))
            left = jnp.concatenate(columns, axis=1)
            if backward:
                term = dot_t(left, jnp.concatenate([weight[i, j, k] for k in range(3)], axis=1))
            else:
                term = dot(left, jnp.concatenate([weight[i, j, k] for k in range(3)], axis=0))
            total = term if total is None else total + term
    return total


def spread_all(height, width, parts, spread):
    at = 0
    for center, edges in parts:
        for t in range(center.shape[0]):
            spread_frame(center[t], edges[t], height, width, spread, at)
            at += (height + 2) * width


def forward_kernel(height, width, x_ref, act, edges, earlier, earlier_edges, weight, out, spread):
    frames = act.shape[0]
    spread_all(height, width, ((earlier, earlier_edges), (act, edges)), spread)
    mixed = conv_sum(height, width, frames, spread, weight, False)
    out[...] = (x_ref[...].astype(F32) + mixed).astype(BF16)


def backward_kernel(
    height, width, x_ref, gain_ref, cot, edges, later, later_edges, weight, out, spread
):
    frames = cot.shape[0]
    spread_all(height, width, ((cot, edges), (later, later_edges)), spread)
    grad_act = conv_sum(height, width, frames, spread, weight, True)
    values = x_ref[...].astype(F32)
    inverse = lax.rsqrt(jnp.mean(values * values, axis=-1, keepdims=True) + EPSILON)
    unit_rms = values * inverse
    gain = gain_ref[...]
    normed = unit_rms * gain
    logistic = jax.nn.sigmoid(normed)
    grad_unit = grad_act * logistic * (1.0 + normed * (1.0 - logistic)) * gain
    grad_norm = inverse * (
        grad_unit - unit_rms * jnp.mean(grad_unit * unit_rms, axis=-1, keepdims=True)
    )
    out[...] = (cot[...].reshape(out.shape).astype(F32) + grad_norm).astype(BF16)


def shape_of(*dims, dtype=BF16):
    return jax.ShapeDtypeStruct(dims, dtype)


def body(features, norm_gain, conv_weight, cotangent):
    frames, height, width, channels = features.shape
    inner = height * width
    cells = frames * inner
    depth, rows_of, cols_of = (lax.axis_size(axis) for axis in AXES)
    chips = rows_of // 2
    owned = channels // (rows_of * cols_of)
    half = channels // 2
    me_t, me_h, me_w = (lax.axis_index(axis) for axis in AXES)
    core, chip = (me_h % 2).astype(jnp.int32).reshape(1), me_h // 2
    flat_x = features.reshape(cells, channels)
    framed_cot = cotangent.reshape(frames, inner, channels)
    gain = norm_gain.reshape(1, channels)
    product = 2 * cells * channels * channels
    size = 2 * cells * channels
    tall = height + CORNERS
    around = 2 * width + 2 * tall

    act, act_t, up, down, lefts, rights = call(
        prepare_kernel,
        (
            shape_of(*features.shape),
            shape_of(channels, cells),
            shape_of(2, frames, width, channels),
            shape_of(2, frames, width, channels),
            shape_of(2, frames, height, channels),
            shape_of(2, frames, height, channels),
        ),
        10 * cells * channels,
        4 * size,
        arrays=3,
    )(features, cotangent, gain)
    framed_act = act.reshape(frames, inner, channels)
    above = shift_line(down, "ha", 1)
    below = shift_line(up, "ha", -1)
    later = shift_line(framed_cot[:2], "ta", -1)
    act_t_other = swap_core(act_t)
    to_left, to_right = call(
        columns_kernel, (shape_of(2, frames, tall, channels),) * 2, 0, size // 2, arrays=4
    )(lefts, rights, above, below)
    left = shift_line(to_right, "wa", 1)
    right = shift_line(to_left, "wa", -1)
    cot_edges, act_edges, mine, send = call(
        functools.partial(bundle_kernel, chips),
        (shape_of(frames, around, channels),) * 2 + (shape_of(frames, inner + around, half),) * 2,
        0,
        3 * size,
        scalars=1,
        arrays=5,
    )(core, framed_cot, above, below, left, right)
    others = swap_core(send)
    later_edges = shift_line(cot_edges[:2], "ta", -1)
    mine_later, send_later = call(
        functools.partial(later_kernel, chips),
        (shape_of(2, inner + around, half),) * 2,
        0,
        2 * size,
        scalars=1,
        arrays=2,
    )(core, later, later_edges)
    others_later = swap_core(send_later)
    earlier = shift_line(framed_act[frames - 2 :], "ta", 1)
    earlier_edges = shift_line(act_edges[frames - 2 :], "ta", 1)

    count = chips * cols_of
    moves = [(du, dw) for du in range(chips) for dw in range(cols_of)]
    places = jnp.stack(
        [((chip + du) % chips) * cols_of + (me_w + dw) % cols_of for du, dw in moves]
    ).astype(jnp.int32)
    spread = pltpu.VMEM((3, frames * (height + 2) * width, half), BF16)
    scratch = (pltpu.VMEM((9, half, channels), F32), spread, spread)
    scale = float(cells * depth * rows_of * cols_of) ** (-0.5)

    def part_of(array, place):
        return lax.dynamic_index_in_dim(array, place, axis=0, keepdims=False)

    gradients = [None] * 3
    for offset in (2, 1, 0):
        bundles = (mine, others) + ((mine_later, others_later) if offset < 2 else ())
        pieces = call(
            functools.partial(taps_kernel, height, width, offset, frames),
            tuple(
                shape_of(9, owned, channels, dtype=F32 if place == 0 else BF16)
                for place in range(count)
            ),
            9 * product,
            4 * size,
            scratch,
            scalars=1,
            arrays=2 + len(bundles),
        )(places, act_t, act_t_other, *bundles)
        total = pieces[0]
        for piece, (du, dw) in zip(pieces[1:], moves[1:]):
            total = total + to_chip(piece, du, dw).astype(F32)
        total = total.reshape(depth, -1, channels)
        rounded = total.astype(BF16)
        piece = part_of(total, me_t)
        for by in range(1, depth):
            piece = piece + ring(part_of(rounded, (me_t + by) % depth), "ta", by).astype(F32)
        piece = (piece * scale).astype(BF16)
        gathered = [ring(piece, "ta", by) for by in range(depth - 1, 0, -1)] + [piece]
        gathered = jnp.roll(jnp.stack(gathered), me_t + 1, axis=0)
        gradients[offset] = gathered.reshape(9, owned, channels)
    grad_weight = jnp.swapaxes(jnp.concatenate(gradients), 1, 2).astype(F32)
    grad_weight = grad_weight.reshape(3, 3, 3, channels, owned)

    spread = pltpu.VMEM((3, (frames + 2) * (height + 2) * width, channels), BF16)
    moved = conv_weight.size * 2 + 4 * size
    decoded = call(
        functools.partial(forward_kernel, height, width),
        shape_of(cells, channels),
        27 * product,
        moved,
        (spread,),
        arrays=6,
    )(flat_x, framed_act, act_edges, earlier, earlier_edges, conv_weight)
    grad_features = call(
        functools.partial(backward_kernel, height, width),
        shape_of(cells, channels),
        27 * product,
        moved,
        (spread,),
        arrays=7,
    )(flat_x, gain, framed_cot, cot_edges, later, later_edges, conv_weight)
    return (
        decoded.reshape(features.shape),
        grad_features.reshape(features.shape),
        grad_weight,
    )


def solution(mesh):
    placed = (P("ta", "ha", "wa", None), P(), P(), P("ta", "ha", "wa", None))
    return jax.shard_map(
        body,
        mesh=mesh,
        in_specs=placed,
        out_specs=(
            P("ta", "ha", "wa", None),
            P("ta", "ha", "wa", None),
            P(None, None, None, None, ("ha", "wa")),
        ),
        check_vma=False,
    )
```

```python
import functools

import jax
import jax.numpy as jnp
from jax import lax
from jax.experimental import pallas as pl
from jax.experimental.pallas import tpu as pltpu
from jax.sharding import PartitionSpec as P

EPSILON = 1e-06
FIRST_TAPS = 10
AXES = ("ta", "ha", "wa")
BF16 = jnp.bfloat16
F32 = jnp.float32


def dot(a, b):
    return jnp.dot(a, b, preferred_element_type=F32)


def dot_t(a, b):
    return lax.dot_general(a, b, (((1,), (1,)), ((), ())), preferred_element_type=F32)


def call(kernel, out_shape, flops, moved, scratch=(), scalars=0, arrays=0, left=0, limit=8):
    specs = [pl.BlockSpec(memory_space=pltpu.SMEM)] * scalars
    specs += [pl.BlockSpec(memory_space=pltpu.VMEM)] * arrays
    specs += [pl.BlockSpec(memory_space=pl.ANY)] * left
    return pl.pallas_call(
        kernel,
        out_shape=out_shape,
        in_specs=specs,
        scratch_shapes=list(scratch),
        compiler_params=pltpu.CompilerParams(vmem_limit_bytes=limit * 2**20),
        cost_estimate=pl.CostEstimate(flops=flops, bytes_accessed=moved, transcendentals=0),
    )


def shift_line(array, axis, by):
    length = lax.axis_size(axis)
    pairs = [(i, i + by) for i in range(length) if 0 <= i + by < length]
    return lax.ppermute(array, axis, pairs)


def swap_core(array):
    length = lax.axis_size("ha")
    return lax.ppermute(array, "ha", [(i, i ^ 1) for i in range(length)])


def swap_pairs(array, axis, odd):
    length = lax.axis_size(axis)
    pairs = []
    for i in range(odd, length - 1, 2):
        pairs += [(i, i + 1), (i + 1, i)]
    return lax.ppermute(array, axis, pairs) if pairs else None


def to_chip(array, du, dw):
    chips, width = lax.axis_size("ha") // 2, lax.axis_size("wa")
    pairs = []
    for u in range(chips):
        for core in range(2):
            for w in range(width):
                source = (2 * u + core) * width + w
                target = (2 * ((u + du) % chips) + core) * width + (w + dw) % width
                pairs.append((source, target))
    return lax.ppermute(array, ("ha", "wa"), pairs)


def ring(array, axis, by):
    length = lax.axis_size(axis)
    return lax.ppermute(array, axis, [(i, (i + by) % length) for i in range(length)])


CORNERS = 16


def prepare_kernel(x_ref, gain_ref, act_ref, act_t_ref, last):
    frames = x_ref.shape[0]
    values = x_ref[...].reshape(-1, x_ref.shape[-1]).astype(F32)
    inverse = lax.rsqrt(jnp.mean(values * values, axis=-1, keepdims=True) + EPSILON)
    normed = values * inverse * gain_ref[...]
    activated = (normed * jax.nn.sigmoid(normed)).astype(BF16)
    act_ref[...] = activated.reshape(x_ref.shape)
    act_t_ref[...] = activated.T
    last[...] = act_ref[frames - 2 :]


def rows_kernel(where_ref, cot, later, earlier, act, for_even, for_odd, lefts, rights):
    _, height, width, _ = cot.shape
    even = where_ref[0] == 0
    for place, refs in enumerate(((cot, later), (earlier, act))):
        at = 0
        for ref in refs:
            to = at + ref.shape[0]
            up, down = ref[:, 0], ref[:, height - 1]
            for_even[place, at:to] = jnp.where(even, down, up)
            for_odd[place, at:to] = jnp.where(even, up, down)
            cells = ref[...].astype(F32)
            lefts[place, at:to] = cells[:, :, 0, :].astype(BF16)
            rights[place, at:to] = cells[:, :, width - 1, :].astype(BF16)
            at = to


def both_sides(is_even, refs, shape):
    by_even = refs[0][...] if len(refs) > 0 else jnp.zeros(shape, BF16)
    by_odd = refs[1][...] if len(refs) > 1 else jnp.zeros(shape, BF16)
    return jnp.where(is_even, by_odd, by_even), jnp.where(is_even, by_even, by_odd)


def columns_kernel(count, where_ref, lefts, rights, *refs):
    swapped, (for_even, for_odd) = refs[:count], refs[count:]
    _, frames, height, channels = lefts.shape
    even_h, even_w = where_ref[0] == 0, where_ref[1] == 0
    width = swapped[0].shape[2]
    above, below = both_sides(even_h, swapped, swapped[0].shape)
    nothing = jnp.zeros((2, frames, CORNERS - 2, channels), F32)
    sides = []
    for source, at in ((lefts, 0), (rights, width - 1)):
        over = above.astype(F32)[:, :, at : at + 1, :]
        under = below.astype(F32)[:, :, at : at + 1, :]
        parts = [source[...].astype(F32), over, under, nothing]
        sides.append(jnp.concatenate(parts, axis=2).astype(BF16))
    for_even[...] = jnp.where(even_w, sides[1], sides[0])
    for_odd[...] = jnp.where(even_w, sides[0], sides[1])


def halves(core, values, chips):
    block = values.shape[-1] // (2 * chips)
    values = values.astype(F32)
    first, second = (
        jnp.concatenate(
            [
                values[..., (2 * u + which) * block : (2 * u + which + 1) * block]
                for u in range(chips)
            ],
            axis=-1,
        )
        for which in range(2)
    )
    own = jnp.where(core == 0, first, second)
    other = jnp.where(core == 0, second, first)
    return own.astype(BF16), other.astype(BF16)


def bundle_kernel(chips, width, counts, where_ref, cot, later, act_t, *refs):
    cot_edges, act_edges, mine, send = refs[sum(counts) :]
    core, even_w = where_ref[0], where_ref[1] == 0
    own, inner, channels = cot.shape
    tall = inner // width + CORNERS
    frames, size, half = mine.shape
    rows = both_sides(core == 0, refs[: counts[0]], (2, frames, width, channels))
    columns = both_sides(even_w, refs[counts[0] : sum(counts)], (2, frames, tall, channels))
    for place, target in enumerate((cot_edges, act_edges)):
        target[...] = jnp.concatenate([side[place] for side in rows + columns], axis=1)
    cells = act_t.shape[1]
    at = cells // half * channels
    for block in range(cells // half):
        send[block * channels : (block + 1) * channels] = act_t[
            :, block * half : (block + 1) * half
        ]
    for t in range(frames):
        inside, inside_send = halves(core, cot[t] if t < own else later[t - own], chips)
        outside, outside_send = halves(core, cot_edges[t], chips)
        mine[t, :inner], mine[t, inner:] = inside, outside
        send[at + t * size : at + t * size + inner] = inside_send
        send[at + t * size + inner : at + (t + 1) * size] = outside_send


def spread_frame(center, edges, height, width, target, at):
    channels = center.shape[-1]
    tall = height + CORNERS
    above, below = edges[:width], edges[width : 2 * width]
    rows = jnp.concatenate([above, center, below], axis=0)
    target[1, at : at + (height + 2) * width, :] = rows
    rows = rows.astype(F32).reshape(height + 2, width, channels)
    place = lax.broadcasted_iota(jnp.int32, rows.shape, 1)
    for k, start, edge, by in ((0, 2 * width, 0, 1), (2, 2 * width + tall, width - 1, width - 1)):
        column = edges[start : start + tall].astype(F32)
        column = jnp.concatenate(
            [column[height : height + 1], column[:height], column[height + 1 : height + 2]], axis=0
        )
        moved = jnp.where(place == edge, column[:, None, :], pltpu.roll(rows, by, 1))
        target[k, at : at + (height + 2) * width, :] = moved.astype(BF16).reshape(-1, channels)


def taps_kernel(height, width, all_taps, *refs):
    inner = height * width
    places, act_a, mine, other, *outs, terms_ref, spread_a, spread_b = refs
    count = len(outs)
    channels, cells = act_a.shape
    frames = cells // inner
    part = terms_ref.shape[1]
    spreads = (spread_a, spread_b)
    step = (height + 2) * width
    blocks = cells // part
    tall = mine.shape[1]
    lowest = 2 - max(tap[0] for tap in all_taps)
    for side, spread in enumerate(spreads):
        for at in range(lowest, frames + 2 - min(tap[0] for tap in all_taps)):
            if side == 0:
                frame = mine[at]
            else:
                start = blocks * channels + at * tall
                frame = other[start : start + tall]
            spread_frame(frame[:inner], frame[inner:], height, width, spread, (at - lowest) * step)
    acts = jnp.concatenate(
        [act_a[...]] + [other[b * channels : (b + 1) * channels] for b in range(blocks)], axis=1
    )

    def shifted(offset, j, k):
        pieces = []
        for spread in spreads:
            for t in range(frames):
                start = (t + 2 - offset - lowest) * step + (2 - j) * width
                pieces.append(spread[2 - k, start : start + inner, :])
        return jnp.concatenate(pieces, axis=0)

    for first in range(0, len(all_taps), 2):
        taps = all_taps[first : first + 2]
        terms = dot(acts, jnp.concatenate([shifted(*tap) for tap in taps], axis=1)).T
        for place in range(len(taps)):
            terms_ref[first + place] = terms[place * part : (place + 1) * part]
    owned = part // count
    for place, out in enumerate(outs):
        start = pl.multiple_of(places[place] * owned, owned)
        out[...] = terms_ref[:, pl.ds(start, owned), :].astype(out.dtype)


def parts_kernel(groups, count, where_ref, *refs):
    total = refs[-1]
    depth, part, channels = total.shape
    outs = refs[-1 - depth : -1]
    rows = total.reshape(depth * part, channels)
    at = 0
    for group in range(groups):
        terms = refs[group * count : (group + 1) * count]
        taps, owned, _ = terms[0].shape
        summed = terms[0][...]
        for term in terms[1:]:
            summed = summed + term[...].astype(F32)
        rows[at : at + taps * owned] = summed.reshape(taps * owned, channels)
        at += taps * owned
    if at < depth * part:
        rows[at:] = jnp.zeros((depth * part - at, channels), F32)
    for place, out in enumerate(outs):
        out[...] = total[where_ref[place]].astype(out.dtype)


def conv_sum(height, width, frames, spread, weight, backward):
    total = None
    for i in range(3):
        for j in range(3):
            at_t, at_h = (2 - i, 2 - j) if backward else (i, j)
            columns = []
            for k in range(3):
                at_w = 2 - k if backward else k
                pieces = []
                for t in range(frames):
                    start = ((t + at_t) * (height + 2) + at_h) * width
                    pieces.append(spread[at_w, start : start + height * width, :])
                columns.append(jnp.concatenate(pieces, axis=0))
            left = jnp.concatenate(columns, axis=1)
            if backward:
                term = dot_t(left, jnp.concatenate([weight[i, j, k] for k in range(3)], axis=1))
            else:
                term = dot(left, jnp.concatenate([weight[i, j, k] for k in range(3)], axis=0))
            total = term if total is None else total + term
    return total


def spread_all(height, width, centers, edges, spread):
    frame = 0
    for center in centers:
        for t in range(center.shape[0]):
            at = frame * (height + 2) * width
            spread_frame(center[t], edges[frame], height, width, spread, at)
            frame += 1


def forward_kernel(height, width, x_ref, earlier, act, edges, weight, after, out, spread):
    frames = act.shape[0]
    spread_all(height, width, (earlier, act), edges, spread)
    mixed = conv_sum(height, width, frames, spread, weight, False)
    out[...] = (x_ref[...].astype(F32) + mixed).astype(BF16)


def backward_kernel(
    height, width, x_ref, gain_ref, cot, later, edges, weight, after, out, spread
):
    frames = cot.shape[0]
    spread_all(height, width, (cot, later), edges, spread)
    grad_act = conv_sum(height, width, frames, spread, weight, True)
    values = x_ref[...].astype(F32)
    inverse = lax.rsqrt(jnp.mean(values * values, axis=-1, keepdims=True) + EPSILON)
    unit_rms = values * inverse
    gain = gain_ref[...]
    normed = unit_rms * gain
    logistic = jax.nn.sigmoid(normed)
    grad_unit = grad_act * logistic * (1.0 + normed * (1.0 - logistic)) * gain
    grad_norm = inverse * (
        grad_unit - unit_rms * jnp.mean(grad_unit * unit_rms, axis=-1, keepdims=True)
    )
    out[...] = (cot[...].reshape(out.shape).astype(F32) + grad_norm).astype(BF16)


def shape_of(*dims, dtype=BF16):
    return jax.ShapeDtypeStruct(dims, dtype)


def body(features, norm_gain, conv_weight, cotangent):
    frames, height, width, channels = features.shape
    inner = height * width
    cells = frames * inner
    depth, rows_of, cols_of = (lax.axis_size(axis) for axis in AXES)
    chips = rows_of // 2
    owned = channels // (rows_of * cols_of)
    half = channels // 2
    me_t, me_h, me_w = (lax.axis_index(axis) for axis in AXES)
    chip = me_h // 2
    where = jnp.stack([me_h % 2, me_w % 2]).astype(jnp.int32)
    flat_x = features.reshape(cells, channels)
    framed_cot = cotangent.reshape(frames, inner, channels)
    gain = norm_gain.reshape(1, channels)
    product = 2 * cells * channels * channels
    size = 2 * cells * channels
    tall = height + CORNERS
    around = 2 * width + 2 * tall

    act, act_t, last = call(
        prepare_kernel,
        (
            shape_of(*features.shape),
            shape_of(channels, cells),
            shape_of(2, *features.shape[1:]),
        ),
        10 * cells * channels,
        2 * size,
        arrays=2,
        limit=12,
    )(features, gain)
    later = shift_line(cotangent[:2], "ta", -1)
    earlier = shift_line(last, "ta", 1)
    for_even, for_odd, lefts, rights = call(
        rows_kernel,
        (
            shape_of(2, frames + 2, width, channels),
            shape_of(2, frames + 2, width, channels),
            shape_of(2, frames + 2, height, channels),
            shape_of(2, frames + 2, height, channels),
        ),
        0,
        2 * size,
        scalars=1,
        arrays=4,
        limit=12,
    )(where, cotangent, later, earlier, act)
    rows = [swap_pairs(for_even, "ha", 0), swap_pairs(for_odd, "ha", 1)]
    rows = [array for array in rows if array is not None]
    for_even, for_odd = call(
        functools.partial(columns_kernel, len(rows)),
        (shape_of(2, frames + 2, tall, channels),) * 2,
        0,
        size // 2,
        scalars=1,
        arrays=2 + len(rows),
    )(where, lefts, rights, *rows)
    columns = [swap_pairs(for_even, "wa", 0), swap_pairs(for_odd, "wa", 1)]
    columns = [array for array in columns if array is not None]
    later = later.reshape(2, inner, channels)
    cot_edges, act_edges, mine, send = call(
        functools.partial(bundle_kernel, chips, width, (len(rows), len(columns))),
        (shape_of(frames + 2, around, channels),) * 2
        + (
            shape_of(frames + 2, inner + around, half),
            shape_of(cells // half * channels + (frames + 2) * (inner + around), half),
        ),
        0,
        3 * size,
        scalars=1,
        arrays=3 + len(rows) + len(columns),
        limit=12,
    )(where, framed_cot, later, act_t, *rows, *columns)
    other = swap_core(send)

    count = chips * cols_of
    moves = [(du, dw) for du in range(chips) for dw in range(cols_of)]
    places = jnp.stack(
        [((chip + du) % chips) * cols_of + (me_w + dw) % cols_of for du, dw in moves]
    ).astype(jnp.int32)
    offsets = [(i, j, k) for i in range(3) for j in range(3) for k in range(3)]
    terms = []
    for taps in (offsets[:FIRST_TAPS], offsets[FIRST_TAPS:]):
        reach = frames + taps[-1][0] - taps[0][0]
        spread = pltpu.VMEM((3, reach * (height + 2) * width, half), BF16)
        pieces = call(
            functools.partial(taps_kernel, height, width, taps),
            tuple(
                shape_of(len(taps), owned, channels, dtype=F32 if place == 0 else BF16)
                for place in range(count)
            ),
            len(taps) * product,
            4 * size,
            (pltpu.VMEM((len(taps), half, channels), F32), spread, spread),
            scalars=1,
            arrays=3,
            limit=24,
        )(places, act_t, mine, other)
        moved = [to_chip(piece, *move) for piece, move in zip(pieces[1:], moves[1:])]
        terms.append([pieces[0]] + moved)
        after = pieces[0]

    framed_act = act.reshape(frames, inner, channels)
    earlier = earlier.reshape(2, inner, channels)
    flat = shape_of(cells, channels)
    spread = pltpu.VMEM((3, (frames + 2) * (height + 2) * width, channels), BF16)
    touched = conv_weight.size * 2 + 4 * size
    grad_features = call(
        functools.partial(backward_kernel, height, width),
        flat,
        27 * product,
        touched,
        (spread,),
        arrays=6,
        left=1,
        limit=24,
    )(flat_x, gain, framed_cot, later, cot_edges, conv_weight, after)
    decoded = call(
        functools.partial(forward_kernel, height, width),
        flat,
        27 * product,
        touched,
        (spread,),
        arrays=5,
        left=1,
        limit=24,
    )(flat_x, earlier, framed_act, act_edges, conv_weight, after)

    part = -(-27 * owned // (16 * depth)) * 16
    owners = jnp.stack([(me_t + by) % depth for by in range(depth)]).astype(jnp.int32)
    own, *sends = call(
        functools.partial(parts_kernel, len(terms), count),
        tuple(
            shape_of(part, channels, dtype=F32 if by == 0 else BF16) for by in range(depth)
        ),
        0,
        2 * size,
        (pltpu.VMEM((depth, part, channels), F32),),
        scalars=1,
        arrays=count * len(terms),
        left=2,
    )(owners, *terms[0], *terms[1], grad_features, decoded)
    for by, sent in enumerate(sends, 1):
        own = own + ring(sent, "ta", by).astype(F32)
    scale = float(cells * depth * rows_of * cols_of) ** (-0.5)
    own = (own * scale).astype(BF16)
    gathered = [ring(own, "ta", by) for by in range(depth - 1, 0, -1)] + [own]
    gathered = jnp.roll(jnp.stack(gathered), me_t + 1, axis=0)
    grad_weight = gathered.reshape(depth * part, channels)[: 27 * owned]
    grad_weight = jnp.swapaxes(grad_weight.reshape(27, owned, channels), 1, 2).astype(F32)
    return (
        decoded.reshape(features.shape),
        grad_features.reshape(features.shape),
        grad_weight.reshape(3, 3, 3, channels, owned),
    )


def solution(mesh):
    placed = (P("ta", "ha", "wa", None), P(), P(), P("ta", "ha", "wa", None))
    return jax.shard_map(
        body,
        mesh=mesh,
        in_specs=placed,
        out_specs=(
            P("ta", "ha", "wa", None),
            P("ta", "ha", "wa", None),
            P(None, None, None, None, ("ha", "wa")),
        ),
        check_vma=False,
    )
```

```python
import functools

import jax
import jax.numpy as jnp
from jax import lax
from jax.experimental import pallas as pl
from jax.experimental.pallas import tpu as pltpu
from jax.sharding import PartitionSpec as P

EPSILON = 1e-06
FIRST_TAPS = 10
AXES = ("ta", "ha", "wa")
BF16 = jnp.bfloat16
F32 = jnp.float32


def dot(a, b):
    return jnp.dot(a, b, preferred_element_type=F32)


def dot_t(a, b):
    return lax.dot_general(a, b, (((1,), (1,)), ((), ())), preferred_element_type=F32)


def call(kernel, out_shape, flops, moved, scratch=(), scalars=0, arrays=0, left=0, limit=8):
    specs = [pl.BlockSpec(memory_space=pltpu.SMEM)] * scalars
    specs += [pl.BlockSpec(memory_space=pltpu.VMEM)] * arrays
    specs += [pl.BlockSpec(memory_space=pl.ANY)] * left
    return pl.pallas_call(
        kernel,
        out_shape=out_shape,
        in_specs=specs,
        scratch_shapes=list(scratch),
        compiler_params=pltpu.CompilerParams(vmem_limit_bytes=limit * 2**20),
        cost_estimate=pl.CostEstimate(flops=flops, bytes_accessed=moved, transcendentals=0),
    )


def shift_line(array, axis, by):
    length = lax.axis_size(axis)
    pairs = [(i, i + by) for i in range(length) if 0 <= i + by < length]
    return lax.ppermute(array, axis, pairs)


def swap_core(array):
    length = lax.axis_size("ha")
    return lax.ppermute(array, "ha", [(i, i ^ 1) for i in range(length)])


def swap_pairs(array, axis, odd):
    length = lax.axis_size(axis)
    pairs = []
    for i in range(odd, length - 1, 2):
        pairs += [(i, i + 1), (i + 1, i)]
    return lax.ppermute(array, axis, pairs) if pairs else None


def to_chip(array, du, dw):
    chips, width = lax.axis_size("ha") // 2, lax.axis_size("wa")
    pairs = []
    for u in range(chips):
        for core in range(2):
            for w in range(width):
                source = (2 * u + core) * width + w
                target = (2 * ((u + du) % chips) + core) * width + (w + dw) % width
                pairs.append((source, target))
    return lax.ppermute(array, ("ha", "wa"), pairs)


def ring(array, axis, by):
    length = lax.axis_size(axis)
    return lax.ppermute(array, axis, [(i, (i + by) % length) for i in range(length)])


CORNERS = 16


def prepare_kernel(x_ref, gain_ref, act_ref, act_t_ref, last):
    frames = x_ref.shape[0]
    values = x_ref[...].reshape(-1, x_ref.shape[-1]).astype(F32)
    inverse = lax.rsqrt(jnp.mean(values * values, axis=-1, keepdims=True) + EPSILON)
    normed = values * inverse * gain_ref[...]
    activated = (normed * jax.nn.sigmoid(normed)).astype(BF16)
    act_ref[...] = activated.reshape(x_ref.shape)
    act_t_ref[...] = activated.T
    last[...] = act_ref[frames - 2 :]


def rows_kernel(where_ref, cot, later, earlier, act, after, for_even, for_odd, lefts, rights):
    _, height, width, _ = cot.shape
    even = where_ref[0] == 0
    for place, refs in enumerate(((cot, later), (earlier, act))):
        at = 0
        for ref in refs:
            to = at + ref.shape[0]
            up, down = ref[:, 0], ref[:, height - 1]
            for_even[place, at:to] = jnp.where(even, down, up)
            for_odd[place, at:to] = jnp.where(even, up, down)
            cells = ref[...].astype(F32)
            lefts[place, at:to] = cells[:, :, 0, :].astype(BF16)
            rights[place, at:to] = cells[:, :, width - 1, :].astype(BF16)
            at = to


def both_sides(is_even, refs, shape):
    shape = refs[0].shape if refs else shape
    by_even = refs[0][...] if len(refs) > 0 else jnp.zeros(shape, BF16)
    by_odd = refs[1][...] if len(refs) > 1 else jnp.zeros(shape, BF16)
    return jnp.where(is_even, by_odd, by_even), jnp.where(is_even, by_even, by_odd)


def columns_kernel(count, slot, where_ref, lefts, rights, *refs):
    swapped, (for_even, for_odd) = refs[:count], refs[count:]
    _, frames, height, channels = lefts.shape
    even_h, even_w = where_ref[0] == 0, where_ref[1] == 0
    width = swapped[0].shape[2]
    above, below = both_sides(even_h, swapped, swapped[0].shape)
    nothing = jnp.zeros((2, slot - frames, channels), F32)
    sides = []
    for source, at in ((lefts, 0), (rights, width - 1)):
        over = above.astype(F32)[:, :, at, :]
        under = below.astype(F32)[:, :, at, :]
        columns = source[...].astype(F32).reshape(2, frames * height, channels)
        parts = [columns, over, nothing, under, nothing]
        sides.append(jnp.concatenate(parts, axis=1).astype(BF16))
    for_even[...] = jnp.where(even_w, sides[1], sides[0])
    for_odd[...] = jnp.where(even_w, sides[0], sides[1])


def halves(core, values, chips):
    block = values.shape[-1] // (2 * chips)
    values = values.astype(F32)
    first, second = (
        jnp.concatenate(
            [
                values[..., (2 * u + which) * block : (2 * u + which + 1) * block]
                for u in range(chips)
            ],
            axis=-1,
        )
        for which in range(2)
    )
    own = jnp.where(core == 0, first, second)
    other = jnp.where(core == 0, second, first)
    return own.astype(BF16), other.astype(BF16)


def own_kernel(chips, where_ref, cot, act_t, mine, send):
    core = where_ref[0]
    frames, inner, half = mine.shape
    channels, cells = act_t.shape
    at = cells // half * channels
    for block in range(cells // half):
        send[block * channels : (block + 1) * channels] = act_t[
            :, block * half : (block + 1) * half
        ]
    for t in range(frames):
        inside, inside_send = halves(core, cot[t], chips)
        mine[t] = inside
        send[at + t * inner : at + (t + 1) * inner] = inside_send


def bundle_kernel(chips, slot, counts, where_ref, later, *refs):
    cot_edges, act_edges, mine, send = refs[sum(counts) :]
    core, even_w = where_ref[0], where_ref[1] == 0
    more, inner, channels = later.shape
    frames, around, _ = cot_edges.shape
    rows = both_sides(core == 0, refs[: counts[0]], None)
    width = rows[0].shape[2]
    height = inner // width
    packed = (2, frames * height + 2 * slot, channels)
    columns = both_sides(even_w, refs[counts[0] : sum(counts)], packed)
    columns = [side.astype(F32) for side in columns]
    nothing = jnp.zeros((frames, CORNERS - 2, channels), F32)
    at = frames * height
    for place, target in enumerate((cot_edges, act_edges)):
        parts = [side[place].astype(F32) for side in rows]
        for side in columns:
            parts.append(side[place, :at].reshape(frames, height, channels))
            parts.append(side[place, at : at + frames][:, None, :])
            parts.append(side[place, at + slot : at + slot + frames][:, None, :])
            parts.append(nothing)
        target[...] = jnp.concatenate(parts, axis=1).astype(BF16)
    for t in range(more):
        inside, inside_send = halves(core, later[t], chips)
        mine[t * inner : (t + 1) * inner] = inside
        send[t * inner : (t + 1) * inner] = inside_send
    at = more * inner
    for t in range(frames):
        outside, outside_send = halves(core, cot_edges[t], chips)
        mine[at + t * around : at + (t + 1) * around] = outside
        send[at + t * around : at + (t + 1) * around] = outside_send


def spread_frame(center, edges, height, width, target, at):
    channels = center.shape[-1]
    tall = height + CORNERS
    above, below = edges[:width], edges[width : 2 * width]
    rows = jnp.concatenate([above, center, below], axis=0)
    target[1, at : at + (height + 2) * width, :] = rows
    rows = rows.astype(F32).reshape(height + 2, width, channels)
    place = lax.broadcasted_iota(jnp.int32, rows.shape, 1)
    for k, start, edge, by in ((0, 2 * width, 0, 1), (2, 2 * width + tall, width - 1, width - 1)):
        column = edges[start : start + tall].astype(F32)
        column = jnp.concatenate(
            [column[height : height + 1], column[:height], column[height + 1 : height + 2]], axis=0
        )
        moved = jnp.where(place == edge, column[:, None, :], pltpu.roll(rows, by, 1))
        target[k, at : at + (height + 2) * width, :] = moved.astype(BF16).reshape(-1, channels)


def taps_kernel(height, width, all_taps, *refs):
    inner = height * width
    places, act_a, *rest = refs
    mine, mine_more, other, other_more, *outs, terms_ref, spread_a, spread_b = rest
    count = len(outs)
    channels, cells = act_a.shape
    frames = cells // inner
    part = terms_ref.shape[1]
    spreads = (spread_a, spread_b)
    step = (height + 2) * width
    blocks = cells // part
    more = 2 * inner
    around = (mine_more.shape[0] - more) // (frames + 2)
    lowest = 2 - max(tap[0] for tap in all_taps)
    for side, spread in enumerate(spreads):
        for at in range(lowest, frames + 2 - min(tap[0] for tap in all_taps)):
            extra = (mine_more, other_more)[side]
            if at >= frames:
                center = extra[(at - frames) * inner : (at - frames + 1) * inner]
            elif side == 0:
                center = mine[at]
            else:
                start = blocks * channels + at * inner
                center = other[start : start + inner]
            edges = extra[more + at * around : more + (at + 1) * around]
            spread_frame(center, edges, height, width, spread, (at - lowest) * step)
    acts = jnp.concatenate(
        [act_a[...]] + [other[b * channels : (b + 1) * channels] for b in range(blocks)], axis=1
    )

    def shifted(offset, j, k):
        pieces = []
        for spread in spreads:
            for t in range(frames):
                start = (t + 2 - offset - lowest) * step + (2 - j) * width
                pieces.append(spread[2 - k, start : start + inner, :])
        return jnp.concatenate(pieces, axis=0)

    for first in range(0, len(all_taps), 2):
        taps = all_taps[first : first + 2]
        terms = dot(acts, jnp.concatenate([shifted(*tap) for tap in taps], axis=1)).T
        for place in range(len(taps)):
            terms_ref[first + place] = terms[place * part : (place + 1) * part]
    owned = part // count
    for place, out in enumerate(outs):
        start = pl.multiple_of(places[place] * owned, owned)
        out[...] = terms_ref[:, pl.ds(start, owned), :].astype(out.dtype)


def parts_kernel(groups, count, where_ref, *refs):
    total = refs[-1]
    depth, part, channels = total.shape
    outs = refs[-1 - depth : -1]
    rows = total.reshape(depth * part, channels)
    at = 0
    for group in range(groups):
        terms = refs[group * count : (group + 1) * count]
        taps, owned, _ = terms[0].shape
        summed = terms[0][...]
        for term in terms[1:]:
            summed = summed + term[...].astype(F32)
        rows[at : at + taps * owned] = summed.reshape(taps * owned, channels)
        at += taps * owned
    if at < depth * part:
        rows[at:] = jnp.zeros((depth * part - at, channels), F32)
    for place, out in enumerate(outs):
        out[...] = total[where_ref[place]].astype(out.dtype)


def conv_sum(height, width, frames, spread, weight, backward):
    total = None
    for i in range(3):
        for j in range(3):
            at_t, at_h = (2 - i, 2 - j) if backward else (i, j)
            columns = []
            for k in range(3):
                at_w = 2 - k if backward else k
                pieces = []
                for t in range(frames):
                    start = ((t + at_t) * (height + 2) + at_h) * width
                    pieces.append(spread[at_w, start : start + height * width, :])
                columns.append(jnp.concatenate(pieces, axis=0))
            left = jnp.concatenate(columns, axis=1)
            if backward:
                term = dot_t(left, jnp.concatenate([weight[i, j, k] for k in range(3)], axis=1))
            else:
                term = dot(left, jnp.concatenate([weight[i, j, k] for k in range(3)], axis=0))
            total = term if total is None else total + term
    return total


def spread_all(height, width, centers, edges, spread):
    frame = 0
    for center in centers:
        for t in range(center.shape[0]):
            at = frame * (height + 2) * width
            spread_frame(center[t], edges[frame], height, width, spread, at)
            frame += 1


def forward_kernel(height, width, x_ref, earlier, act, edges, weight, after, out, token, spread):
    frames = act.shape[0]
    token[...] = jnp.zeros_like(token)
    spread_all(height, width, (earlier, act), edges, spread)
    mixed = conv_sum(height, width, frames, spread, weight, False)
    out[...] = (x_ref[...].astype(F32) + mixed).astype(BF16)


def backward_kernel(
    height, width, x_ref, gain_ref, cot, later, edges, weight, after, out, token, spread
):
    frames = cot.shape[0]
    token[...] = jnp.zeros_like(token)
    spread_all(height, width, (cot, later), edges, spread)
    grad_act = conv_sum(height, width, frames, spread, weight, True)
    values = x_ref[...].astype(F32)
    inverse = lax.rsqrt(jnp.mean(values * values, axis=-1, keepdims=True) + EPSILON)
    unit_rms = values * inverse
    gain = gain_ref[...]
    normed = unit_rms * gain
    logistic = jax.nn.sigmoid(normed)
    grad_unit = grad_act * logistic * (1.0 + normed * (1.0 - logistic)) * gain
    grad_norm = inverse * (
        grad_unit - unit_rms * jnp.mean(grad_unit * unit_rms, axis=-1, keepdims=True)
    )
    out[...] = (cot[...].reshape(out.shape).astype(F32) + grad_norm).astype(BF16)


def shape_of(*dims, dtype=BF16):
    return jax.ShapeDtypeStruct(dims, dtype)


def body(features, norm_gain, conv_weight, cotangent):
    frames, height, width, channels = features.shape
    inner = height * width
    cells = frames * inner
    depth, rows_of, cols_of = (lax.axis_size(axis) for axis in AXES)
    chips = rows_of // 2
    owned = channels // (rows_of * cols_of)
    half = channels // 2
    me_t, me_h, me_w = (lax.axis_index(axis) for axis in AXES)
    chip = me_h // 2
    where = jnp.stack([me_h % 2, me_w % 2]).astype(jnp.int32)
    flat_x = features.reshape(cells, channels)
    slot = -(-(frames + 2) // 8) * 8
    framed_cot = cotangent.reshape(frames, inner, channels)
    gain = norm_gain.reshape(1, channels)
    product = 2 * cells * channels * channels
    size = 2 * cells * channels
    tall = height + CORNERS
    around = 2 * width + 2 * tall

    act, act_t, last = call(
        prepare_kernel,
        (
            shape_of(*features.shape),
            shape_of(channels, cells),
            shape_of(2, *features.shape[1:]),
        ),
        10 * cells * channels,
        2 * size,
        arrays=2,
        limit=12,
    )(features, gain)
    later = shift_line(cotangent[:2], "ta", -1)
    earlier = shift_line(last, "ta", 1)
    mine, send = call(
        functools.partial(own_kernel, chips),
        (
            shape_of(frames, inner, half),
            shape_of(cells // half * channels + cells, half),
        ),
        0,
        2 * size,
        scalars=1,
        arrays=2,
        limit=12,
    )(where, framed_cot, act_t)
    other = swap_core(send)
    for_even, for_odd, lefts, rights = call(
        rows_kernel,
        (
            shape_of(2, frames + 2, width, channels),
            shape_of(2, frames + 2, width, channels),
            shape_of(2, frames + 2, height, channels),
            shape_of(2, frames + 2, height, channels),
        ),
        0,
        2 * size,
        scalars=1,
        arrays=4,
        left=1,
        limit=12,
    )(where, cotangent, later, earlier, act, other)
    rows = [swap_pairs(for_even, "ha", 0), swap_pairs(for_odd, "ha", 1)]
    rows = [array for array in rows if array is not None]
    for_even, for_odd = call(
        functools.partial(columns_kernel, len(rows), slot),
        (shape_of(2, (frames + 2) * height + 2 * slot, channels),) * 2,
        0,
        size // 2,
        scalars=1,
        arrays=2 + len(rows),
    )(where, lefts, rights, *rows)
    columns = [swap_pairs(for_even, "wa", 0), swap_pairs(for_odd, "wa", 1)]
    columns = [array for array in columns if array is not None]
    later = later.reshape(2, inner, channels)
    cot_edges, act_edges, mine_more, send_more = call(
        functools.partial(bundle_kernel, chips, slot, (len(rows), len(columns))),
        (shape_of(frames + 2, around, channels),) * 2
        + (shape_of(2 * inner + (frames + 2) * around, half),) * 2,
        0,
        size,
        scalars=1,
        arrays=1 + len(rows) + len(columns),
        limit=12,
    )(where, later, *rows, *columns)
    other_more = swap_core(send_more)

    count = chips * cols_of
    moves = [(du, dw) for du in range(chips) for dw in range(cols_of)]
    places = jnp.stack(
        [((chip + du) % chips) * cols_of + (me_w + dw) % cols_of for du, dw in moves]
    ).astype(jnp.int32)
    offsets = [(i, j, k) for i in range(3) for j in range(3) for k in range(3)]
    terms = []
    for taps in (offsets[:FIRST_TAPS], offsets[FIRST_TAPS:]):
        reach = frames + taps[-1][0] - taps[0][0]
        spread = pltpu.VMEM((3, reach * (height + 2) * width, half), BF16)
        pieces = call(
            functools.partial(taps_kernel, height, width, taps),
            tuple(
                shape_of(len(taps), owned, channels, dtype=F32 if place == 0 else BF16)
                for place in range(count)
            ),
            len(taps) * product,
            4 * size,
            (pltpu.VMEM((len(taps), half, channels), F32), spread, spread),
            scalars=1,
            arrays=5,
            limit=16,
        )(places, act_t, mine, mine_more, other, other_more)
        moved = [to_chip(piece, *move) for piece, move in zip(pieces[1:], moves[1:])]
        terms.append([pieces[0]] + moved)
        after = pieces[0]

    framed_act = act.reshape(frames, inner, channels)
    earlier = earlier.reshape(2, inner, channels)
    flat = (shape_of(cells, channels), shape_of(8, 128, dtype=F32))
    spread = pltpu.VMEM((3, (frames + 2) * (height + 2) * width, channels), BF16)
    touched = conv_weight.size * 2 + 4 * size
    grad_features, token_a = call(
        functools.partial(backward_kernel, height, width),
        flat,
        27 * product,
        touched,
        (spread,),
        arrays=6,
        left=1,
        limit=16,
    )(flat_x, gain, framed_cot, later, cot_edges, conv_weight, after)
    decoded, token_b = call(
        functools.partial(forward_kernel, height, width),
        flat,
        27 * product,
        touched,
        (spread,),
        arrays=5,
        left=1,
        limit=16,
    )(flat_x, earlier, framed_act, act_edges, conv_weight, after)

    part = -(-27 * owned // (16 * depth)) * 16
    owners = jnp.stack([(me_t + by) % depth for by in range(depth)]).astype(jnp.int32)
    own, *sends = call(
        functools.partial(parts_kernel, len(terms), count),
        tuple(
            shape_of(part, channels, dtype=F32 if by == 0 else BF16) for by in range(depth)
        ),
        0,
        2 * size,
        (pltpu.VMEM((depth, part, channels), F32),),
        scalars=1,
        arrays=count * len(terms),
        left=2,
    )(owners, *terms[0], *terms[1], token_a, token_b)
    for by, sent in enumerate(sends, 1):
        own = own + ring(sent, "ta", by).astype(F32)
    scale = float(cells * depth * rows_of * cols_of) ** (-0.5)
    own = (own * scale).astype(BF16)
    gathered = [ring(own, "ta", by) for by in range(depth - 1, 0, -1)] + [own]
    gathered = jnp.roll(jnp.stack(gathered), me_t + 1, axis=0)
    grad_weight = gathered.reshape(depth * part, channels)[: 27 * owned]
    grad_weight = jnp.swapaxes(grad_weight.reshape(27, owned, channels), 1, 2).astype(F32)
    return (
        decoded.reshape(features.shape),
        grad_features.reshape(features.shape),
        grad_weight.reshape(3, 3, 3, channels, owned),
    )


def solution(mesh):
    placed = (P("ta", "ha", "wa", None), P(), P(), P("ta", "ha", "wa", None))
    return jax.shard_map(
        body,
        mesh=mesh,
        in_specs=placed,
        out_specs=(
            P("ta", "ha", "wa", None),
            P("ta", "ha", "wa", None),
            P(None, None, None, None, ("ha", "wa")),
        ),
        check_vma=False,
    )
```

```python
import functools

import jax
import jax.numpy as jnp
from jax import lax
from jax.experimental import pallas as pl
from jax.experimental.pallas import tpu as pltpu
from jax.sharding import PartitionSpec as P

EPSILON = 1e-06
FIRST_TAPS = 8
AXES = ("ta", "ha", "wa")
BF16 = jnp.bfloat16
F32 = jnp.float32


def dot(a, b):
    return jnp.dot(a, b, preferred_element_type=F32)


def dot_t(a, b):
    return lax.dot_general(a, b, (((1,), (1,)), ((), ())), preferred_element_type=F32)


def call(kernel, out_shape, flops, moved, scratch=(), scalars=0, arrays=0, left=0, limit=8):
    specs = [pl.BlockSpec(memory_space=pltpu.SMEM)] * scalars
    specs += [pl.BlockSpec(memory_space=pltpu.VMEM)] * arrays
    specs += [pl.BlockSpec(memory_space=pl.ANY)] * left
    return pl.pallas_call(
        kernel,
        out_shape=out_shape,
        in_specs=specs,
        scratch_shapes=list(scratch),
        compiler_params=pltpu.CompilerParams(vmem_limit_bytes=limit * 2**20),
        cost_estimate=pl.CostEstimate(flops=flops, bytes_accessed=moved, transcendentals=0),
    )


def shift_line(array, axis, by):
    length = lax.axis_size(axis)
    pairs = [(i, i + by) for i in range(length) if 0 <= i + by < length]
    return lax.ppermute(array, axis, pairs)


def swap_core(array):
    length = lax.axis_size("ha")
    return lax.ppermute(array, "ha", [(i, i ^ 1) for i in range(length)])


def swap_pairs(array, axis, odd):
    length = lax.axis_size(axis)
    pairs = []
    for i in range(odd, length - 1, 2):
        pairs += [(i, i + 1), (i + 1, i)]
    return lax.ppermute(array, axis, pairs) if pairs else None


def to_chip(array, du, dw):
    chips, width = lax.axis_size("ha") // 2, lax.axis_size("wa")
    pairs = []
    for u in range(chips):
        for core in range(2):
            for w in range(width):
                source = (2 * u + core) * width + w
                target = (2 * ((u + du) % chips) + core) * width + (w + dw) % width
                pairs.append((source, target))
    return lax.ppermute(array, ("ha", "wa"), pairs)


def partner(place, by, length):
    return place ^ by if length & (length - 1) == 0 else (place + by) % length


def to_partner(array, axis, by):
    length = lax.axis_size(axis)
    return lax.ppermute(array, axis, [(i, partner(i, by, length)) for i in range(length)])


CORNERS = 16


def prepare_kernel(where_ref, x_ref, gain_ref, cot_ref, act_ref, act_t_ref, for_even, for_odd, kept):
    frames = x_ref.shape[0]
    values = x_ref[...].reshape(-1, x_ref.shape[-1]).astype(F32)
    inverse = lax.rsqrt(jnp.mean(values * values, axis=-1, keepdims=True) + EPSILON)
    normed = values * inverse * gain_ref[...]
    activated = (normed * jax.nn.sigmoid(normed)).astype(BF16)
    act_ref[...] = activated.reshape(x_ref.shape)
    act_t_ref[...] = activated.T
    kept[...] = cot_ref[...]
    last, first = act_ref[frames - 2 :], cot_ref[:2]
    even = where_ref[2] == 0
    for_even[...] = jnp.where(even, last, first)
    for_odd[...] = jnp.where(even, first, last)


def rows_kernel(count, where_ref, cot, act, *refs):
    met = refs[:count]
    later, earlier, for_even, for_odd, lefts, rights = refs[-6:]
    earlier[...], later[...] = both_sides(where_ref[2] == 0, met, later.shape)
    _, height, width, _ = cot.shape
    even = where_ref[0] == 0
    for place, refs in enumerate(((cot, later), (earlier, act))):
        at = 0
        for ref in refs:
            to = at + ref.shape[0]
            up, down = ref[:, 0], ref[:, height - 1]
            for_even[place, at:to] = jnp.where(even, down, up)
            for_odd[place, at:to] = jnp.where(even, up, down)
            cells = ref[...].astype(F32)
            lefts[place, at:to] = cells[:, :, 0, :].astype(BF16)
            rights[place, at:to] = cells[:, :, width - 1, :].astype(BF16)
            at = to


def both_sides(is_even, refs, shape):
    shape = refs[0].shape if refs else shape
    by_even = refs[0][...] if len(refs) > 0 else jnp.zeros(shape, BF16)
    by_odd = refs[1][...] if len(refs) > 1 else jnp.zeros(shape, BF16)
    return jnp.where(is_even, by_odd, by_even), jnp.where(is_even, by_even, by_odd)


def columns_kernel(count, slot, where_ref, lefts, rights, *refs):
    swapped, (for_even, for_odd) = refs[:count], refs[-2:]
    _, frames, height, channels = lefts.shape
    even_h, even_w = where_ref[0] == 0, where_ref[1] == 0
    width = swapped[0].shape[2]
    above, below = both_sides(even_h, swapped, swapped[0].shape)
    nothing = jnp.zeros((2, slot - frames, channels), F32)
    sides = []
    for source, at in ((lefts, 0), (rights, width - 1)):
        over = above.astype(F32)[:, :, at, :]
        under = below.astype(F32)[:, :, at, :]
        columns = source[...].astype(F32).reshape(2, frames * height, channels)
        parts = [columns, over, nothing, under, nothing]
        sides.append(jnp.concatenate(parts, axis=1).astype(BF16))
    for_even[...] = jnp.where(even_w, sides[1], sides[0])
    for_odd[...] = jnp.where(even_w, sides[0], sides[1])


def halves(core, values, chips):
    block = values.shape[-1] // (2 * chips)
    values = values.astype(F32)
    first, second = (
        jnp.concatenate(
            [
                values[..., (2 * u + which) * block : (2 * u + which + 1) * block]
                for u in range(chips)
            ],
            axis=-1,
        )
        for which in range(2)
    )
    own = jnp.where(core == 0, first, second)
    other = jnp.where(core == 0, second, first)
    return own.astype(BF16), other.astype(BF16)


def own_kernel(chips, where_ref, cot, act_t, after, mine, send):
    core = where_ref[0]
    frames, inner, half = mine.shape
    channels, cells = act_t.shape
    at = cells // half * channels
    for block in range(cells // half):
        send[block * channels : (block + 1) * channels] = act_t[
            :, block * half : (block + 1) * half
        ]
    for t in range(frames):
        inside, inside_send = halves(core, cot[t], chips)
        mine[t] = inside
        send[at + t * inner : at + (t + 1) * inner] = inside_send


def bundle_kernel(chips, slot, counts, where_ref, later, *refs):
    cot_edges, act_edges, mine, send = refs[sum(counts) :]
    core, even_w = where_ref[0], where_ref[1] == 0
    more, inner, channels = later.shape
    frames, around, _ = cot_edges.shape
    rows = both_sides(core == 0, refs[: counts[0]], None)
    width = rows[0].shape[2]
    height = inner // width
    packed = (2, frames * height + 2 * slot, channels)
    columns = both_sides(even_w, refs[counts[0] : sum(counts)], packed)
    columns = [side.astype(F32) for side in columns]
    nothing = jnp.zeros((frames, CORNERS - 2, channels), F32)
    at = frames * height
    for place, target in enumerate((cot_edges, act_edges)):
        parts = [side[place].astype(F32) for side in rows]
        for side in columns:
            parts.append(side[place, :at].reshape(frames, height, channels))
            parts.append(side[place, at : at + frames][:, None, :])
            parts.append(side[place, at + slot : at + slot + frames][:, None, :])
            parts.append(nothing)
        target[...] = jnp.concatenate(parts, axis=1).astype(BF16)
    for t in range(more):
        inside, inside_send = halves(core, later[t], chips)
        mine[t * inner : (t + 1) * inner] = inside
        send[t * inner : (t + 1) * inner] = inside_send
    at = more * inner
    for t in range(frames):
        outside, outside_send = halves(core, cot_edges[t], chips)
        mine[at + t * around : at + (t + 1) * around] = outside
        send[at + t * around : at + (t + 1) * around] = outside_send


def spread_frame(center, edges, height, width, target, at):
    channels = center.shape[-1]
    tall = height + CORNERS
    above, below = edges[:width], edges[width : 2 * width]
    rows = jnp.concatenate([above, center, below], axis=0)
    target[1, at : at + (height + 2) * width, :] = rows
    rows = rows.astype(F32).reshape(height + 2, width, channels)
    place = lax.broadcasted_iota(jnp.int32, rows.shape, 1)
    for k, start, edge, by in ((0, 2 * width, 0, 1), (2, 2 * width + tall, width - 1, width - 1)):
        column = edges[start : start + tall].astype(F32)
        column = jnp.concatenate(
            [column[height : height + 1], column[:height], column[height + 1 : height + 2]], axis=0
        )
        moved = jnp.where(place == edge, column[:, None, :], pltpu.roll(rows, by, 1))
        target[k, at : at + (height + 2) * width, :] = moved.astype(BF16).reshape(-1, channels)


def taps_kernel(height, width, all_taps, *refs):
    inner = height * width
    places, act_a, *rest = refs
    mine, mine_more, other, other_more, *outs, terms_ref, spread_a, spread_b = rest
    count = len(outs)
    channels, cells = act_a.shape
    frames = cells // inner
    part = terms_ref.shape[1]
    spreads = (spread_a, spread_b)
    step = (height + 2) * width
    blocks = cells // part
    more = 2 * inner
    around = (mine_more.shape[0] - more) // (frames + 2)
    lowest = 2 - max(tap[0] for tap in all_taps)
    for side, spread in enumerate(spreads):
        for at in range(lowest, frames + 2 - min(tap[0] for tap in all_taps)):
            extra = (mine_more, other_more)[side]
            if at >= frames:
                center = extra[(at - frames) * inner : (at - frames + 1) * inner]
            elif side == 0:
                center = mine[at]
            else:
                start = blocks * channels + at * inner
                center = other[start : start + inner]
            edges = extra[more + at * around : more + (at + 1) * around]
            spread_frame(center, edges, height, width, spread, (at - lowest) * step)
    acts = jnp.concatenate(
        [act_a[...]] + [other[b * channels : (b + 1) * channels] for b in range(blocks)], axis=1
    )

    def shifted(offset, j, k):
        pieces = []
        for spread in spreads:
            for t in range(frames):
                start = (t + 2 - offset - lowest) * step + (2 - j) * width
                pieces.append(spread[2 - k, start : start + inner, :])
        return jnp.concatenate(pieces, axis=0)

    for first in range(0, len(all_taps), 2):
        taps = all_taps[first : first + 2]
        terms = dot(acts, jnp.concatenate([shifted(*tap) for tap in taps], axis=1)).T
        for place in range(len(taps)):
            terms_ref[first + place] = terms[place * part : (place + 1) * part]
    owned = part // count
    for place, out in enumerate(outs):
        start = pl.multiple_of(places[place] * owned, owned)
        out[...] = terms_ref[:, pl.ds(start, owned), :].astype(out.dtype)


def parts_kernel(groups, count, where_ref, *refs):
    total = refs[-1]
    depth, part, channels = total.shape
    outs = refs[-1 - depth : -1]
    rows = total.reshape(depth * part, channels)
    at = 0
    for group in range(groups):
        terms = refs[group * count : (group + 1) * count]
        taps, owned, _ = terms[0].shape
        summed = terms[0][...]
        for term in terms[1:]:
            summed = summed + term[...].astype(F32)
        rows[at : at + taps * owned] = summed.reshape(taps * owned, channels)
        at += taps * owned
    if at < depth * part:
        rows[at:] = jnp.zeros((depth * part - at, channels), F32)
    for place, out in enumerate(outs):
        out[...] = total[where_ref[place]].astype(out.dtype)


def conv_sum(height, width, frames, spread, weight, backward):
    total = None
    for i in range(3):
        for j in range(3):
            at_t, at_h = (2 - i, 2 - j) if backward else (i, j)
            columns = []
            for k in range(3):
                at_w = 2 - k if backward else k
                pieces = []
                for t in range(frames):
                    start = ((t + at_t) * (height + 2) + at_h) * width
                    pieces.append(spread[at_w, start : start + height * width, :])
                columns.append(jnp.concatenate(pieces, axis=0))
            left = jnp.concatenate(columns, axis=1)
            if backward:
                term = dot_t(left, jnp.concatenate([weight[i, j, k] for k in range(3)], axis=1))
            else:
                term = dot(left, jnp.concatenate([weight[i, j, k] for k in range(3)], axis=0))
            total = term if total is None else total + term
    return total


def spread_all(height, width, centers, edges, spread):
    frame = 0
    for center in centers:
        for t in range(center.shape[0]):
            at = frame * (height + 2) * width
            spread_frame(center[t], edges[frame], height, width, spread, at)
            frame += 1


def forward_kernel(height, width, x_ref, earlier, act, edges, weight, after, out, token, spread):
    frames = act.shape[0]
    token[...] = jnp.zeros_like(token)
    spread_all(height, width, (earlier, act), edges, spread)
    mixed = conv_sum(height, width, frames, spread, weight, False)
    out[...] = (x_ref[...].astype(F32) + mixed).astype(BF16)


def backward_kernel(
    height, width, x_ref, gain_ref, cot, later, edges, weight, after, out, token, spread
):
    frames = cot.shape[0]
    token[...] = jnp.zeros_like(token)
    spread_all(height, width, (cot, later), edges, spread)
    grad_act = conv_sum(height, width, frames, spread, weight, True)
    values = x_ref[...].astype(F32)
    inverse = lax.rsqrt(jnp.mean(values * values, axis=-1, keepdims=True) + EPSILON)
    unit_rms = values * inverse
    gain = gain_ref[...]
    normed = unit_rms * gain
    logistic = jax.nn.sigmoid(normed)
    grad_unit = grad_act * logistic * (1.0 + normed * (1.0 - logistic)) * gain
    grad_norm = inverse * (
        grad_unit - unit_rms * jnp.mean(grad_unit * unit_rms, axis=-1, keepdims=True)
    )
    out[...] = (cot[...].reshape(out.shape).astype(F32) + grad_norm).astype(BF16)


def shape_of(*dims, dtype=BF16):
    return jax.ShapeDtypeStruct(dims, dtype)


def body(features, norm_gain, conv_weight, cotangent):
    frames, height, width, channels = features.shape
    inner = height * width
    cells = frames * inner
    depth, rows_of, cols_of = (lax.axis_size(axis) for axis in AXES)
    chips = rows_of // 2
    owned = channels // (rows_of * cols_of)
    half = channels // 2
    me_t, me_h, me_w = (lax.axis_index(axis) for axis in AXES)
    chip = me_h // 2
    where = jnp.stack([me_h % 2, me_w % 2, me_t % 2]).astype(jnp.int32)
    flat_x = features.reshape(cells, channels)
    slot = -(-(frames + 2) // 8) * 8
    framed_cot = cotangent.reshape(frames, inner, channels)
    gain = norm_gain.reshape(1, channels)
    product = 2 * cells * channels * channels
    size = 2 * cells * channels
    tall = height + CORNERS
    around = 2 * width + 2 * tall

    act, act_t, for_even, for_odd, kept = call(
        prepare_kernel,
        (
            shape_of(*features.shape),
            shape_of(channels, cells),
            shape_of(2, *features.shape[1:]),
            shape_of(2, *features.shape[1:]),
            shape_of(*features.shape),
        ),
        10 * cells * channels,
        3 * size,
        scalars=1,
        arrays=3,
        limit=12,
    )(where, features, gain, cotangent)
    met = [swap_pairs(for_even, "ta", 0), swap_pairs(for_odd, "ta", 1)]
    met = [array for array in met if array is not None]
    later, earlier, for_even, for_odd, lefts, rights = call(
        functools.partial(rows_kernel, len(met)),
        (
            shape_of(2, *features.shape[1:]),
            shape_of(2, *features.shape[1:]),
            shape_of(2, frames + 2, width, channels),
            shape_of(2, frames + 2, width, channels),
            shape_of(2, frames + 2, height, channels),
            shape_of(2, frames + 2, height, channels),
        ),
        0,
        2 * size,
        scalars=1,
        arrays=2 + len(met),
        limit=12,
    )(where, kept, act, *met)
    mine, send = call(
        functools.partial(own_kernel, chips),
        (
            shape_of(frames, inner, half),
            shape_of(cells // half * channels + cells, half),
        ),
        0,
        2 * size,
        scalars=1,
        arrays=2,
        left=1,
        limit=12,
    )(where, kept.reshape(framed_cot.shape), act_t, for_even)
    other = swap_core(send)
    rows = [swap_pairs(for_even, "ha", 0), swap_pairs(for_odd, "ha", 1)]
    rows = [array for array in rows if array is not None]
    for_even, for_odd = call(
        functools.partial(columns_kernel, len(rows), slot),
        (shape_of(2, (frames + 2) * height + 2 * slot, channels),) * 2,
        0,
        size // 2,
        scalars=1,
        arrays=2 + len(rows),
        left=1,
    )(where, lefts, rights, *rows, other)
    columns = [swap_pairs(for_even, "wa", 0), swap_pairs(for_odd, "wa", 1)]
    columns = [array for array in columns if array is not None]
    later = later.reshape(2, inner, channels)
    cot_edges, act_edges, mine_more, send_more = call(
        functools.partial(bundle_kernel, chips, slot, (len(rows), len(columns))),
        (shape_of(frames + 2, around, channels),) * 2
        + (shape_of(2 * inner + (frames + 2) * around, half),) * 2,
        0,
        size,
        scalars=1,
        arrays=1 + len(rows) + len(columns),
        limit=12,
    )(where, later, *rows, *columns)
    other_more = swap_core(send_more)

    count = chips * cols_of
    moves = [(du, dw) for du in range(chips) for dw in range(cols_of)]
    places = jnp.stack(
        [((chip + du) % chips) * cols_of + (me_w + dw) % cols_of for du, dw in moves]
    ).astype(jnp.int32)
    offsets = [(i, j, k) for i in range(3) for j in range(3) for k in range(3)]
    terms = []
    for taps in (offsets[:FIRST_TAPS], offsets[FIRST_TAPS:]):
        reach = frames + taps[-1][0] - taps[0][0]
        spread = pltpu.VMEM((3, reach * (height + 2) * width, half), BF16)
        pieces = call(
            functools.partial(taps_kernel, height, width, taps),
            tuple(
                shape_of(len(taps), owned, channels, dtype=F32 if place == 0 else BF16)
                for place in range(count)
            ),
            len(taps) * product,
            4 * size,
            (pltpu.VMEM((len(taps), half, channels), F32), spread, spread),
            scalars=1,
            arrays=5,
            limit=16,
        )(places, act_t, mine, mine_more, other, other_more)
        moved = [to_chip(piece, *move) for piece, move in zip(pieces[1:], moves[1:])]
        terms.append([pieces[0]] + moved)
        after = pieces[0]

    framed_act = act.reshape(frames, inner, channels)
    earlier = earlier.reshape(2, inner, channels)
    flat = (shape_of(cells, channels), shape_of(8, 128, dtype=F32))
    spread = pltpu.VMEM((3, (frames + 2) * (height + 2) * width, channels), BF16)
    touched = conv_weight.size * 2 + 4 * size
    grad_features, token_a = call(
        functools.partial(backward_kernel, height, width),
        flat,
        27 * product,
        touched,
        (spread,),
        arrays=6,
        left=1,
        limit=16,
    )(flat_x, gain, framed_cot, later, cot_edges, conv_weight, after)
    decoded, token_b = call(
        functools.partial(forward_kernel, height, width),
        flat,
        27 * product,
        touched,
        (spread,),
        arrays=5,
        left=1,
        limit=16,
    )(flat_x, earlier, framed_act, act_edges, conv_weight, after)

    part = -(-27 * owned // (16 * depth)) * 16
    owners = jnp.stack([partner(me_t, by, depth) for by in range(depth)]).astype(jnp.int32)
    own, *sends = call(
        functools.partial(parts_kernel, len(terms), count),
        tuple(
            shape_of(part, channels, dtype=F32 if by == 0 else BF16) for by in range(depth)
        ),
        0,
        2 * size,
        (pltpu.VMEM((depth, part, channels), F32),),
        scalars=1,
        arrays=count * len(terms),
        left=2,
    )(owners, *terms[0], *terms[1], token_a, token_b)
    for by, sent in enumerate(sends, 1):
        own = own + to_partner(sent, "ta", by).astype(F32)
    scale = float(cells * depth * rows_of * cols_of) ** (-0.5)
    own = (own * scale).astype(BF16)
    gathered = jnp.stack([own] + [to_partner(own, "ta", by) for by in range(1, depth)])
    if depth & (depth - 1) == 0:
        places = [me_t ^ rank for rank in range(depth)]
    else:
        places = [(me_t - rank) % depth for rank in range(depth)]
    gathered = jnp.concatenate(
        [lax.dynamic_index_in_dim(gathered, place, axis=0) for place in places]
    )
    grad_weight = gathered.reshape(depth * part, channels)[: 27 * owned]
    grad_weight = jnp.swapaxes(grad_weight.reshape(27, owned, channels), 1, 2).astype(F32)
    return (
        decoded.reshape(features.shape),
        grad_features.reshape(features.shape),
        grad_weight.reshape(3, 3, 3, channels, owned),
    )


def solution(mesh):
    placed = (P("ta", "ha", "wa", None), P(), P(), P("ta", "ha", "wa", None))
    return jax.shard_map(
        body,
        mesh=mesh,
        in_specs=placed,
        out_specs=(
            P("ta", "ha", "wa", None),
            P("ta", "ha", "wa", None),
            P(None, None, None, None, ("ha", "wa")),
        ),
        check_vma=False,
    )
```

```python
import functools

import jax
import jax.numpy as jnp
from jax import lax
from jax.experimental import pallas as pl
from jax.experimental.pallas import tpu as pltpu
from jax.sharding import PartitionSpec as P

EPSILON = 1e-06
FIRST_TAPS = 11
AXES = ("ta", "ha", "wa")
BF16 = jnp.bfloat16
F32 = jnp.float32


def dot(a, b):
    return jnp.dot(a, b, preferred_element_type=F32)


def dot_t(a, b):
    return lax.dot_general(a, b, (((1,), (1,)), ((), ())), preferred_element_type=F32)


def call(kernel, out_shape, flops, moved, scratch=(), scalars=0, arrays=0, left=0, limit=8):
    specs = [pl.BlockSpec(memory_space=pltpu.SMEM)] * scalars
    specs += [pl.BlockSpec(memory_space=pltpu.VMEM)] * arrays
    specs += [pl.BlockSpec(memory_space=pl.ANY)] * left
    return pl.pallas_call(
        kernel,
        out_shape=out_shape,
        in_specs=specs,
        scratch_shapes=list(scratch),
        compiler_params=pltpu.CompilerParams(vmem_limit_bytes=limit * 2**20),
        cost_estimate=pl.CostEstimate(flops=flops, bytes_accessed=moved, transcendentals=0),
    )


def shift_line(array, axis, by):
    length = lax.axis_size(axis)
    pairs = [(i, i + by) for i in range(length) if 0 <= i + by < length]
    return lax.ppermute(array, axis, pairs)


def swap_core(array):
    length = lax.axis_size("ha")
    return lax.ppermute(array, "ha", [(i, i ^ 1) for i in range(length)])


def swap_pairs(array, axis, odd):
    length = lax.axis_size(axis)
    pairs = []
    for i in range(odd, length - 1, 2):
        pairs += [(i, i + 1), (i + 1, i)]
    return lax.ppermute(array, axis, pairs) if pairs else None


def to_chip(array, du, dw):
    chips, width = lax.axis_size("ha") // 2, lax.axis_size("wa")
    pairs = []
    for u in range(chips):
        for core in range(2):
            for w in range(width):
                source = (2 * u + core) * width + w
                target = (2 * ((u + du) % chips) + core) * width + (w + dw) % width
                pairs.append((source, target))
    return lax.ppermute(array, ("ha", "wa"), pairs)


def partner(place, by, length):
    return place ^ by if length & (length - 1) == 0 else (place + by) % length


def to_partner(array, axis, by):
    length = lax.axis_size(axis)
    return lax.ppermute(array, axis, [(i, partner(i, by, length)) for i in range(length)])


CORNERS = 16


def prepare_kernel(where_ref, x_ref, gain_ref, cot_ref, act_ref, act_t_ref, for_even, for_odd, kept):
    frames = x_ref.shape[0]
    values = x_ref[...].reshape(-1, x_ref.shape[-1]).astype(F32)
    inverse = lax.rsqrt(jnp.mean(values * values, axis=-1, keepdims=True) + EPSILON)
    normed = values * inverse * gain_ref[...]
    activated = (normed * jax.nn.sigmoid(normed)).astype(BF16)
    act_ref[...] = activated.reshape(x_ref.shape)
    act_t_ref[...] = activated.T
    kept[...] = cot_ref[...]
    last, first = act_ref[frames - 2 :], cot_ref[:2]
    even = where_ref[2] == 0
    for_even[...] = jnp.where(even, last, first)
    for_odd[...] = jnp.where(even, first, last)


def rows_kernel(count, where_ref, cot, act, *refs):
    met = refs[:count]
    later, earlier, for_even, for_odd, lefts, rights = refs[-6:]
    earlier[...], later[...] = both_sides(where_ref[2] == 0, met, later.shape)
    _, height, width, _ = cot.shape
    even = where_ref[0] == 0
    for place, refs in enumerate(((cot, later), (earlier, act))):
        at = 0
        for ref in refs:
            to = at + ref.shape[0]
            up, down = ref[:, 0], ref[:, height - 1]
            for_even[place, at:to] = jnp.where(even, down, up)
            for_odd[place, at:to] = jnp.where(even, up, down)
            cells = ref[...].astype(F32)
            lefts[place, at:to] = cells[:, :, 0, :].astype(BF16)
            rights[place, at:to] = cells[:, :, width - 1, :].astype(BF16)
            at = to


def both_sides(is_even, refs, shape):
    shape = refs[0].shape if refs else shape
    by_even = refs[0][...] if len(refs) > 0 else jnp.zeros(shape, BF16)
    by_odd = refs[1][...] if len(refs) > 1 else jnp.zeros(shape, BF16)
    return jnp.where(is_even, by_odd, by_even), jnp.where(is_even, by_even, by_odd)


def columns_kernel(count, slot, where_ref, lefts, rights, *refs):
    swapped, targets = refs[:count], refs[count + 1 :]
    _, frames, height, channels = lefts.shape
    even_h, even_w = where_ref[0] == 0, where_ref[1] == 0
    width = swapped[0].shape[2]
    above, below = both_sides(even_h, swapped, swapped[0].shape)
    nothing = jnp.zeros((2, slot - frames, channels), F32)
    shape = (2, frames * height, channels)
    first, last = lefts[...].reshape(shape), rights[...].reshape(shape)
    for target, (one, other) in zip(targets, ((last, first), (first, last))):
        target[:, : frames * height] = jnp.where(even_w, one, other)
    corners = []
    for at in (0, width - 1):
        over = above.astype(F32)[:, :, at, :]
        under = below.astype(F32)[:, :, at, :]
        corners.append(jnp.concatenate([over, nothing, under, nothing], axis=1))
    for target, (one, other) in zip(targets, (corners[::-1], corners)):
        target[:, frames * height :] = jnp.where(even_w, one, other).astype(BF16)


def halves(core, values, chips):
    block = values.shape[-1] // (2 * chips)
    values = values.astype(F32)
    first, second = (
        jnp.concatenate(
            [
                values[..., (2 * u + which) * block : (2 * u + which + 1) * block]
                for u in range(chips)
            ],
            axis=-1,
        )
        for which in range(2)
    )
    own = jnp.where(core == 0, first, second)
    other = jnp.where(core == 0, second, first)
    return own.astype(BF16), other.astype(BF16)


def own_kernel(chips, where_ref, cot, act_t, after, mine, send):
    core = where_ref[0]
    frames, inner, half = mine.shape
    channels, cells = act_t.shape
    at = cells // half * channels
    for block in range(cells // half):
        send[block * channels : (block + 1) * channels] = act_t[
            :, block * half : (block + 1) * half
        ]
    for t in range(frames):
        inside, inside_send = halves(core, cot[t], chips)
        mine[t] = inside
        send[at + t * inner : at + (t + 1) * inner] = inside_send


def bundle_kernel(chips, slot, counts, where_ref, later, *refs):
    cot_edges, act_edges, mine, send = refs[sum(counts) :]
    core, even_w = where_ref[0], where_ref[1] == 0
    more, inner, channels = later.shape
    frames, around, _ = cot_edges.shape
    rows = both_sides(core == 0, refs[: counts[0]], None)
    width = rows[0].shape[2]
    height = inner // width
    packed = (2, frames * height + 2 * slot, channels)
    columns = both_sides(even_w, refs[counts[0] : sum(counts)], packed)
    columns = [side.astype(F32) for side in columns]
    nothing = jnp.zeros((frames, CORNERS - 2, channels), F32)
    at = frames * height
    for place, target in enumerate((cot_edges, act_edges)):
        parts = [side[place].astype(F32) for side in rows]
        for side in columns:
            parts.append(side[place, :at].reshape(frames, height, channels))
            parts.append(side[place, at : at + frames][:, None, :])
            parts.append(side[place, at + slot : at + slot + frames][:, None, :])
            parts.append(nothing)
        target[...] = jnp.concatenate(parts, axis=1).astype(BF16)
    for t in range(more):
        inside, inside_send = halves(core, later[t], chips)
        mine[t * inner : (t + 1) * inner] = inside
        send[t * inner : (t + 1) * inner] = inside_send
    at = more * inner
    for t in range(frames):
        outside, outside_send = halves(core, cot_edges[t], chips)
        mine[at + t * around : at + (t + 1) * around] = outside
        send[at + t * around : at + (t + 1) * around] = outside_send


def spread_frame(center, edges, height, width, target, at):
    channels = center.shape[-1]
    tall = height + CORNERS
    above, below = edges[:width], edges[width : 2 * width]
    rows = jnp.concatenate([above, center, below], axis=0)
    target[1, at : at + (height + 2) * width, :] = rows
    rows = rows.astype(F32).reshape(height + 2, width, channels)
    place = lax.broadcasted_iota(jnp.int32, rows.shape, 1)
    for k, start, edge, by in ((0, 2 * width, 0, 1), (2, 2 * width + tall, width - 1, width - 1)):
        column = edges[start : start + tall].astype(F32)
        column = jnp.concatenate(
            [column[height : height + 1], column[:height], column[height + 1 : height + 2]], axis=0
        )
        moved = jnp.where(place == edge, column[:, None, :], pltpu.roll(rows, by, 1))
        target[k, at : at + (height + 2) * width, :] = moved.astype(BF16).reshape(-1, channels)


def taps_kernel(height, width, all_taps, *refs):
    inner = height * width
    places, act_a, *rest = refs
    mine, mine_more, other, other_more, *outs, terms_ref, spread_a, spread_b = rest
    count = len(outs)
    channels, cells = act_a.shape
    frames = cells // inner
    part = terms_ref.shape[1]
    spreads = (spread_a, spread_b)
    step = (height + 2) * width
    blocks = cells // part
    more = 2 * inner
    around = (mine_more.shape[0] - more) // (frames + 2)
    lowest = 2 - max(tap[0] for tap in all_taps)
    for side, spread in enumerate(spreads):
        for at in range(lowest, frames + 2 - min(tap[0] for tap in all_taps)):
            extra = (mine_more, other_more)[side]
            if at >= frames:
                center = extra[(at - frames) * inner : (at - frames + 1) * inner]
            elif side == 0:
                center = mine[at]
            else:
                start = blocks * channels + at * inner
                center = other[start : start + inner]
            edges = extra[more + at * around : more + (at + 1) * around]
            spread_frame(center, edges, height, width, spread, (at - lowest) * step)
    acts = jnp.concatenate(
        [act_a[...]] + [other[b * channels : (b + 1) * channels] for b in range(blocks)], axis=1
    )

    def shifted(offset, j, k):
        pieces = []
        for spread in spreads:
            for t in range(frames):
                start = (t + 2 - offset - lowest) * step + (2 - j) * width
                pieces.append(spread[2 - k, start : start + inner, :])
        return jnp.concatenate(pieces, axis=0)

    for first in range(0, len(all_taps), 2):
        taps = all_taps[first : first + 2]
        terms = dot(acts, jnp.concatenate([shifted(*tap) for tap in taps], axis=1)).T
        for place in range(len(taps)):
            terms_ref[first + place] = terms[place * part : (place + 1) * part]
    owned = part // count
    for place, out in enumerate(outs):
        start = pl.multiple_of(places[place] * owned, owned)
        out[...] = terms_ref[:, pl.ds(start, owned), :].astype(out.dtype)


def parts_kernel(groups, count, where_ref, *refs):
    total = refs[-1]
    depth, part, channels = total.shape
    outs = refs[-1 - depth : -1]
    rows = total.reshape(depth * part, channels)
    at = 0
    for group in range(groups):
        terms = refs[group * count : (group + 1) * count]
        taps, owned, _ = terms[0].shape
        summed = terms[0][...]
        for term in terms[1:]:
            summed = summed + term[...].astype(F32)
        rows[at : at + taps * owned] = summed.reshape(taps * owned, channels)
        at += taps * owned
    if at < depth * part:
        rows[at:] = jnp.zeros((depth * part - at, channels), F32)
    for place, out in enumerate(outs):
        out[...] = total[where_ref[place]].astype(out.dtype)


def conv_sum(height, width, frames, spread, weight, backward):
    total = None
    for i in range(3):
        for j in range(3):
            at_t, at_h = (2 - i, 2 - j) if backward else (i, j)
            columns = []
            for k in range(3):
                at_w = 2 - k if backward else k
                pieces = []
                for t in range(frames):
                    start = ((t + at_t) * (height + 2) + at_h) * width
                    pieces.append(spread[at_w, start : start + height * width, :])
                columns.append(jnp.concatenate(pieces, axis=0))
            left = jnp.concatenate(columns, axis=1)
            if backward:
                term = dot_t(left, jnp.concatenate([weight[i, j, k] for k in range(3)], axis=1))
            else:
                term = dot(left, jnp.concatenate([weight[i, j, k] for k in range(3)], axis=0))
            total = term if total is None else total + term
    return total


def spread_all(height, width, centers, edges, spread):
    frame = 0
    for center in centers:
        for t in range(center.shape[0]):
            at = frame * (height + 2) * width
            spread_frame(center[t], edges[frame], height, width, spread, at)
            frame += 1


def forward_kernel(height, width, x_ref, earlier, act, edges, weight, after, out, token, spread):
    frames = act.shape[0]
    token[...] = jnp.zeros_like(token)
    spread_all(height, width, (earlier, act), edges, spread)
    mixed = conv_sum(height, width, frames, spread, weight, False)
    out[...] = (x_ref[...].astype(F32) + mixed).astype(BF16)


def backward_kernel(
    height, width, x_ref, gain_ref, cot, later, edges, weight, after, out, token, spread
):
    frames = cot.shape[0]
    token[...] = jnp.zeros_like(token)
    spread_all(height, width, (cot, later), edges, spread)
    grad_act = conv_sum(height, width, frames, spread, weight, True)
    values = x_ref[...].astype(F32)
    inverse = lax.rsqrt(jnp.mean(values * values, axis=-1, keepdims=True) + EPSILON)
    unit_rms = values * inverse
    gain = gain_ref[...]
    normed = unit_rms * gain
    logistic = jax.nn.sigmoid(normed)
    grad_unit = grad_act * logistic * (1.0 + normed * (1.0 - logistic)) * gain
    grad_norm = inverse * (
        grad_unit - unit_rms * jnp.mean(grad_unit * unit_rms, axis=-1, keepdims=True)
    )
    out[...] = (cot[...].reshape(out.shape).astype(F32) + grad_norm).astype(BF16)


def shape_of(*dims, dtype=BF16):
    return jax.ShapeDtypeStruct(dims, dtype)


def body(features, norm_gain, conv_weight, cotangent):
    frames, height, width, channels = features.shape
    inner = height * width
    cells = frames * inner
    depth, rows_of, cols_of = (lax.axis_size(axis) for axis in AXES)
    chips = rows_of // 2
    owned = channels // (rows_of * cols_of)
    half = channels // 2
    me_t, me_h, me_w = (lax.axis_index(axis) for axis in AXES)
    chip = me_h // 2
    where = jnp.stack([me_h % 2, me_w % 2, me_t % 2]).astype(jnp.int32)
    flat_x = features.reshape(cells, channels)
    slot = -(-(frames + 2) // 8) * 8
    framed_cot = cotangent.reshape(frames, inner, channels)
    gain = norm_gain.reshape(1, channels)
    product = 2 * cells * channels * channels
    size = 2 * cells * channels
    tall = height + CORNERS
    around = 2 * width + 2 * tall

    act, act_t, for_even, for_odd, kept = call(
        prepare_kernel,
        (
            shape_of(*features.shape),
            shape_of(channels, cells),
            shape_of(2, *features.shape[1:]),
            shape_of(2, *features.shape[1:]),
            shape_of(*features.shape),
        ),
        10 * cells * channels,
        3 * size,
        scalars=1,
        arrays=3,
        limit=12,
    )(where, features, gain, cotangent)
    met = [swap_pairs(for_even, "ta", 0), swap_pairs(for_odd, "ta", 1)]
    met = [array for array in met if array is not None]
    later, earlier, for_even, for_odd, lefts, rights = call(
        functools.partial(rows_kernel, len(met)),
        (
            shape_of(2, *features.shape[1:]),
            shape_of(2, *features.shape[1:]),
            shape_of(2, frames + 2, width, channels),
            shape_of(2, frames + 2, width, channels),
            shape_of(2, frames + 2, height, channels),
            shape_of(2, frames + 2, height, channels),
        ),
        0,
        2 * size,
        scalars=1,
        arrays=2 + len(met),
        limit=12,
    )(where, kept, act, *met)
    mine, send = call(
        functools.partial(own_kernel, chips),
        (
            shape_of(frames, inner, half),
            shape_of(cells // half * channels + cells, half),
        ),
        0,
        2 * size,
        scalars=1,
        arrays=2,
        left=1,
        limit=12,
    )(where, kept.reshape(framed_cot.shape), act_t, for_even)
    other = swap_core(send)
    rows = [swap_pairs(for_even, "ha", 0), swap_pairs(for_odd, "ha", 1)]
    rows = [array for array in rows if array is not None]
    by_swap = call(
        functools.partial(columns_kernel, len(rows), slot),
        (shape_of(2, (frames + 2) * height + 2 * slot, channels),) * min(2, cols_of - 1),
        0,
        size // 2,
        scalars=1,
        arrays=2 + len(rows),
        left=1,
    )(where, lefts, rights, *rows, other)
    columns = [swap_pairs(array, "wa", odd) for odd, array in enumerate(by_swap)]
    later = later.reshape(2, inner, channels)
    cot_edges, act_edges, mine_more, send_more = call(
        functools.partial(bundle_kernel, chips, slot, (len(rows), len(columns))),
        (shape_of(frames + 2, around, channels),) * 2
        + (shape_of(2 * inner + (frames + 2) * around, half),) * 2,
        0,
        size,
        scalars=1,
        arrays=1 + len(rows) + len(columns),
        limit=12,
    )(where, later, *rows, *columns)
    other_more = swap_core(send_more)

    count = chips * cols_of
    moves = [(du, dw) for du in range(chips) for dw in range(cols_of)]
    places = jnp.stack(
        [((chip + du) % chips) * cols_of + (me_w + dw) % cols_of for du, dw in moves]
    ).astype(jnp.int32)
    offsets = [(i, j, k) for i in range(3) for j in range(3) for k in range(3)]
    terms = []
    for taps in (offsets[:FIRST_TAPS], offsets[FIRST_TAPS:]):
        reach = frames + taps[-1][0] - taps[0][0]
        spread = pltpu.VMEM((3, reach * (height + 2) * width, half), BF16)
        pieces = call(
            functools.partial(taps_kernel, height, width, taps),
            tuple(
                shape_of(len(taps), owned, channels, dtype=F32 if place == 0 else BF16)
                for place in range(count)
            ),
            len(taps) * product,
            4 * size,
            (pltpu.VMEM((len(taps), half, channels), F32), spread, spread),
            scalars=1,
            arrays=5,
            limit=16,
        )(places, act_t, mine, mine_more, other, other_more)
        moved = [to_chip(piece, *move) for piece, move in zip(pieces[1:], moves[1:])]
        terms.append([pieces[0]] + moved)
        after = pieces[0]

    framed_act = act.reshape(frames, inner, channels)
    earlier = earlier.reshape(2, inner, channels)
    flat = (shape_of(cells, channels), shape_of(8, 128, dtype=F32))
    spread = pltpu.VMEM((3, (frames + 2) * (height + 2) * width, channels), BF16)
    touched = conv_weight.size * 2 + 4 * size
    grad_features, token_a = call(
        functools.partial(backward_kernel, height, width),
        flat,
        27 * product,
        touched,
        (spread,),
        arrays=6,
        left=1,
        limit=16,
    )(flat_x, gain, framed_cot, later, cot_edges, conv_weight, after)
    decoded, token_b = call(
        functools.partial(forward_kernel, height, width),
        flat,
        27 * product,
        touched,
        (spread,),
        arrays=5,
        left=1,
        limit=16,
    )(flat_x, earlier, framed_act, act_edges, conv_weight, after)

    part = -(-27 * owned // (16 * depth)) * 16
    owners = jnp.stack([partner(me_t, by, depth) for by in range(depth)]).astype(jnp.int32)
    own, *sends = call(
        functools.partial(parts_kernel, len(terms), count),
        tuple(
            shape_of(part, channels, dtype=F32 if by == 0 else BF16) for by in range(depth)
        ),
        0,
        2 * size,
        (pltpu.VMEM((depth, part, channels), F32),),
        scalars=1,
        arrays=count * len(terms),
        left=2,
    )(owners, *terms[0], *terms[1], token_a, token_b)
    for by, sent in enumerate(sends, 1):
        own = own + to_partner(sent, "ta", by).astype(F32)
    scale = float(cells * depth * rows_of * cols_of) ** (-0.5)
    own = (own * scale).astype(BF16)
    gathered = jnp.stack([own] + [to_partner(own, "ta", by) for by in range(1, depth)])
    if depth & (depth - 1) == 0:
        places = [me_t ^ rank for rank in range(depth)]
    else:
        places = [(me_t - rank) % depth for rank in range(depth)]
    gathered = jnp.concatenate(
        [lax.dynamic_index_in_dim(gathered, place, axis=0) for place in places]
    )
    grad_weight = gathered.reshape(depth * part, channels)[: 27 * owned]
    grad_weight = jnp.swapaxes(grad_weight.reshape(27, owned, channels), 1, 2).astype(F32)
    return (
        decoded.reshape(features.shape),
        grad_features.reshape(features.shape),
        grad_weight.reshape(3, 3, 3, channels, owned),
    )


def solution(mesh):
    placed = (P("ta", "ha", "wa", None), P(), P(), P("ta", "ha", "wa", None))
    return jax.shard_map(
        body,
        mesh=mesh,
        in_specs=placed,
        out_specs=(
            P("ta", "ha", "wa", None),
            P("ta", "ha", "wa", None),
            P(None, None, None, None, ("ha", "wa")),
        ),
        check_vma=False,
    )
```

```python
import functools

import jax
import jax.numpy as jnp
from jax import lax
from jax.experimental import pallas as pl
from jax.experimental.pallas import tpu as pltpu
from jax.sharding import PartitionSpec as P

EPSILON = 1e-06
FIRST_TAPS = 12
AXES = ("ta", "ha", "wa")
BF16 = jnp.bfloat16
F32 = jnp.float32


def dot(a, b):
    return jnp.dot(a, b, preferred_element_type=F32)


def dot_t(a, b):
    return lax.dot_general(a, b, (((1,), (1,)), ((), ())), preferred_element_type=F32)


def call(kernel, out_shape, flops, moved, scratch=(), scalars=0, arrays=0, left=0, limit=8):
    specs = [pl.BlockSpec(memory_space=pltpu.SMEM)] * scalars
    specs += [pl.BlockSpec(memory_space=pltpu.VMEM)] * arrays
    specs += [pl.BlockSpec(memory_space=pl.ANY)] * left
    return pl.pallas_call(
        kernel,
        out_shape=out_shape,
        in_specs=specs,
        scratch_shapes=list(scratch),
        compiler_params=pltpu.CompilerParams(vmem_limit_bytes=limit * 2**20),
        cost_estimate=pl.CostEstimate(flops=flops, bytes_accessed=moved, transcendentals=0),
    )


def shift_line(array, axis, by):
    length = lax.axis_size(axis)
    pairs = [(i, i + by) for i in range(length) if 0 <= i + by < length]
    return lax.ppermute(array, axis, pairs)


def swap_core(array):
    length = lax.axis_size("ha")
    return lax.ppermute(array, "ha", [(i, i ^ 1) for i in range(length)])


def swap_pairs(array, axis, odd):
    length = lax.axis_size(axis)
    pairs = []
    for i in range(odd, length - 1, 2):
        pairs += [(i, i + 1), (i + 1, i)]
    return lax.ppermute(array, axis, pairs) if pairs else None


def to_chip(array, du, dw):
    chips, width = lax.axis_size("ha") // 2, lax.axis_size("wa")
    pairs = []
    for u in range(chips):
        for core in range(2):
            for w in range(width):
                source = (2 * u + core) * width + w
                target = (2 * ((u + du) % chips) + core) * width + (w + dw) % width
                pairs.append((source, target))
    return lax.ppermute(array, ("ha", "wa"), pairs)


def partner(place, by, length):
    return place ^ by if length & (length - 1) == 0 else (place + by) % length


def to_partner(array, axis, by):
    length = lax.axis_size(axis)
    return lax.ppermute(array, axis, [(i, partner(i, by, length)) for i in range(length)])


CORNERS = 16


def prepare_kernel(where_ref, x_ref, gain_ref, cot_ref, act_ref, act_t_ref, for_even, for_odd, kept):
    frames = x_ref.shape[0]
    values = x_ref[...].reshape(-1, x_ref.shape[-1]).astype(F32)
    inverse = lax.rsqrt(jnp.mean(values * values, axis=-1, keepdims=True) + EPSILON)
    normed = values * inverse * gain_ref[...]
    activated = (normed * jax.nn.sigmoid(normed)).astype(BF16)
    act_ref[...] = activated.reshape(x_ref.shape)
    act_t_ref[...] = activated.T
    kept[...] = cot_ref[...]
    last, first = act_ref[frames - 2 :], cot_ref[:2]
    even = where_ref[2] == 0
    for_even[...] = jnp.where(even, last, first)
    for_odd[...] = jnp.where(even, first, last)


def rows_kernel(count, where_ref, cot, act, *refs):
    met = refs[:count]
    later, earlier, for_even, for_odd, lefts, rights = refs[-6:]
    earlier[...], later[...] = both_sides(where_ref[2] == 0, met, later.shape)
    _, height, width, _ = cot.shape
    even = where_ref[0] == 0
    for place, refs in enumerate(((cot, later), (earlier, act))):
        at = 0
        for ref in refs:
            to = at + ref.shape[0]
            up, down = ref[:, 0], ref[:, height - 1]
            for_even[place, at:to] = jnp.where(even, down, up)
            for_odd[place, at:to] = jnp.where(even, up, down)
            cells = ref[...].astype(F32)
            lefts[place, at:to] = cells[:, :, 0, :].astype(BF16)
            rights[place, at:to] = cells[:, :, width - 1, :].astype(BF16)
            at = to


def both_sides(is_even, refs, shape):
    shape = refs[0].shape if refs else shape
    by_even = refs[0][...] if len(refs) > 0 else jnp.zeros(shape, BF16)
    by_odd = refs[1][...] if len(refs) > 1 else jnp.zeros(shape, BF16)
    return jnp.where(is_even, by_odd, by_even), jnp.where(is_even, by_even, by_odd)


def columns_kernel(count, slot, where_ref, lefts, rights, *refs):
    swapped, mine = refs[:count], refs[count]
    kept, *targets = refs[count + 2 :]
    kept[...] = mine[...]
    _, frames, height, channels = lefts.shape
    even_h, even_w = where_ref[0] == 0, where_ref[1] == 0
    width = swapped[0].shape[2]
    above, below = both_sides(even_h, swapped, swapped[0].shape)
    nothing = jnp.zeros((2, slot - frames, channels), F32)
    shape = (2, frames * height, channels)
    first, last = lefts[...].reshape(shape), rights[...].reshape(shape)
    for target, (one, other) in zip(targets, ((last, first), (first, last))):
        target[:, : frames * height] = jnp.where(even_w, one, other)
    corners = []
    for at in (0, width - 1):
        over = above.astype(F32)[:, :, at, :]
        under = below.astype(F32)[:, :, at, :]
        corners.append(jnp.concatenate([over, nothing, under, nothing], axis=1))
    for target, (one, other) in zip(targets, (corners[::-1], corners)):
        target[:, frames * height :] = jnp.where(even_w, one, other).astype(BF16)


def halves(core, values, chips):
    block = values.shape[-1] // (2 * chips)
    values = values.astype(F32)
    first, second = (
        jnp.concatenate(
            [
                values[..., (2 * u + which) * block : (2 * u + which + 1) * block]
                for u in range(chips)
            ],
            axis=-1,
        )
        for which in range(2)
    )
    own = jnp.where(core == 0, first, second)
    other = jnp.where(core == 0, second, first)
    return own.astype(BF16), other.astype(BF16)


def own_kernel(chips, where_ref, cot, act_t, after, mine, send):
    core = where_ref[0]
    frames, inner, half = mine.shape
    channels, cells = act_t.shape
    at = cells // half * channels
    for block in range(cells // half):
        send[block * channels : (block + 1) * channels] = act_t[
            :, block * half : (block + 1) * half
        ]
    for t in range(frames):
        inside, inside_send = halves(core, cot[t], chips)
        mine[t] = inside
        send[at + t * inner : at + (t + 1) * inner] = inside_send


def bundle_kernel(chips, slot, counts, where_ref, later, mine_own, *refs):
    cot_edges, act_edges, mine, send = refs[sum(counts) :]
    skip = mine.shape[0] - send.shape[0]
    mine[:skip] = mine_own[...].reshape(skip, mine.shape[1])
    core, even_w = where_ref[0], where_ref[1] == 0
    more, inner, channels = later.shape
    frames, around, _ = cot_edges.shape
    rows = both_sides(core == 0, refs[: counts[0]], None)
    width = rows[0].shape[2]
    height = inner // width
    packed = (2, frames * height + 2 * slot, channels)
    columns = both_sides(even_w, refs[counts[0] : sum(counts)], packed)
    columns = [side.astype(F32) for side in columns]
    nothing = jnp.zeros((frames, CORNERS - 2, channels), F32)
    at = frames * height
    for place, target in enumerate((cot_edges, act_edges)):
        parts = [side[place].astype(F32) for side in rows]
        for side in columns:
            parts.append(side[place, :at].reshape(frames, height, channels))
            parts.append(side[place, at : at + frames][:, None, :])
            parts.append(side[place, at + slot : at + slot + frames][:, None, :])
            parts.append(nothing)
        target[...] = jnp.concatenate(parts, axis=1).astype(BF16)
    for t in range(more):
        inside, inside_send = halves(core, later[t], chips)
        mine[skip + t * inner : skip + (t + 1) * inner] = inside
        send[t * inner : (t + 1) * inner] = inside_send
    at = more * inner
    for t in range(frames):
        outside, outside_send = halves(core, cot_edges[t], chips)
        mine[skip + at + t * around : skip + at + (t + 1) * around] = outside
        send[at + t * around : at + (t + 1) * around] = outside_send


def spread_frame(center, edges, height, width, target, at):
    channels = center.shape[-1]
    tall = height + CORNERS
    above, below = edges[:width], edges[width : 2 * width]
    rows = jnp.concatenate([above, center, below], axis=0)
    target[1, at : at + (height + 2) * width, :] = rows
    rows = rows.astype(F32).reshape(height + 2, width, channels)
    place = lax.broadcasted_iota(jnp.int32, rows.shape, 1)
    for k, start, edge, by in ((0, 2 * width, 0, 1), (2, 2 * width + tall, width - 1, width - 1)):
        column = edges[start : start + tall].astype(F32)
        column = jnp.concatenate(
            [column[height : height + 1], column[:height], column[height + 1 : height + 2]], axis=0
        )
        moved = jnp.where(place == edge, column[:, None, :], pltpu.roll(rows, by, 1))
        target[k, at : at + (height + 2) * width, :] = moved.astype(BF16).reshape(-1, channels)


def taps_kernel(height, width, all_taps, *refs):
    inner = height * width
    places, act_a, *rest = refs
    mine, other, other_more, *outs, terms_ref, spread_a, spread_b = rest
    count = len(outs)
    channels, cells = act_a.shape
    frames = cells // inner
    part = terms_ref.shape[1]
    spreads = (spread_a, spread_b)
    step = (height + 2) * width
    blocks = cells // part
    around = mine.shape[0] // (frames + 2) - inner
    lowest = 2 - max(tap[0] for tap in all_taps)
    for side, spread in enumerate(spreads):
        for at in range(lowest, frames + 2 - min(tap[0] for tap in all_taps)):
            if side == 0:
                center = mine[at * inner : (at + 1) * inner]
                start = (frames + 2) * inner + at * around
                edges = mine[start : start + around]
            else:
                start = blocks * channels + at * inner
                center = (
                    other[start : start + inner]
                    if at < frames
                    else other_more[(at - frames) * inner : (at - frames + 1) * inner]
                )
                start = 2 * inner + at * around
                edges = other_more[start : start + around]
            spread_frame(center, edges, height, width, spread, (at - lowest) * step)
    acts = jnp.concatenate(
        [act_a[...]] + [other[b * channels : (b + 1) * channels] for b in range(blocks)], axis=1
    )

    def shifted(offset, j, k):
        pieces = []
        for spread in spreads:
            for t in range(frames):
                start = (t + 2 - offset - lowest) * step + (2 - j) * width
                pieces.append(spread[2 - k, start : start + inner, :])
        return jnp.concatenate(pieces, axis=0)

    for first in range(0, len(all_taps), 2):
        taps = all_taps[first : first + 2]
        terms = dot(acts, jnp.concatenate([shifted(*tap) for tap in taps], axis=1)).T
        for place in range(len(taps)):
            terms_ref[first + place] = terms[place * part : (place + 1) * part]
    owned = part // count
    for place, out in enumerate(outs):
        start = pl.multiple_of(places[place] * owned, owned)
        out[...] = terms_ref[:, pl.ds(start, owned), :].astype(out.dtype)


def parts_kernel(groups, count, where_ref, *refs):
    total = refs[-1]
    depth, part, channels = total.shape
    outs = refs[-1 - depth : -1]
    rows = total.reshape(depth * part, channels)
    at = 0
    for group in range(groups):
        terms = refs[group * count : (group + 1) * count]
        taps, owned, _ = terms[0].shape
        summed = terms[0][...]
        for term in terms[1:]:
            summed = summed + term[...].astype(F32)
        rows[at : at + taps * owned] = summed.reshape(taps * owned, channels)
        at += taps * owned
    if at < depth * part:
        rows[at:] = jnp.zeros((depth * part - at, channels), F32)
    for place, out in enumerate(outs):
        out[...] = total[where_ref[place]].astype(out.dtype)


def conv_sum(height, width, frames, spread, weight, backward):
    total = None
    for i in range(3):
        for j in range(3):
            at_t, at_h = (2 - i, 2 - j) if backward else (i, j)
            columns = []
            for k in range(3):
                at_w = 2 - k if backward else k
                pieces = []
                for t in range(frames):
                    start = ((t + at_t) * (height + 2) + at_h) * width
                    pieces.append(spread[at_w, start : start + height * width, :])
                columns.append(jnp.concatenate(pieces, axis=0))
            left = jnp.concatenate(columns, axis=1)
            if backward:
                term = dot_t(left, jnp.concatenate([weight[i, j, k] for k in range(3)], axis=1))
            else:
                term = dot(left, jnp.concatenate([weight[i, j, k] for k in range(3)], axis=0))
            total = term if total is None else total + term
    return total


def spread_all(height, width, centers, edges, spread):
    frame = 0
    for center in centers:
        for t in range(center.shape[0]):
            at = frame * (height + 2) * width
            spread_frame(center[t], edges[frame], height, width, spread, at)
            frame += 1


def forward_kernel(height, width, x_ref, earlier, act, edges, weight, after, out, token, spread):
    frames = act.shape[0]
    token[...] = jnp.zeros_like(token)
    spread_all(height, width, (earlier, act), edges, spread)
    mixed = conv_sum(height, width, frames, spread, weight, False)
    out[...] = (x_ref[...].astype(F32) + mixed).astype(BF16)


def backward_kernel(
    height, width, x_ref, gain_ref, cot, later, edges, weight, after, out, token, spread
):
    frames = cot.shape[0]
    token[...] = jnp.zeros_like(token)
    spread_all(height, width, (cot, later), edges, spread)
    grad_act = conv_sum(height, width, frames, spread, weight, True)
    values = x_ref[...].astype(F32)
    inverse = lax.rsqrt(jnp.mean(values * values, axis=-1, keepdims=True) + EPSILON)
    unit_rms = values * inverse
    gain = gain_ref[...]
    normed = unit_rms * gain
    logistic = jax.nn.sigmoid(normed)
    grad_unit = grad_act * logistic * (1.0 + normed * (1.0 - logistic)) * gain
    grad_norm = inverse * (
        grad_unit - unit_rms * jnp.mean(grad_unit * unit_rms, axis=-1, keepdims=True)
    )
    out[...] = (cot[...].reshape(out.shape).astype(F32) + grad_norm).astype(BF16)


def shape_of(*dims, dtype=BF16):
    return jax.ShapeDtypeStruct(dims, dtype)


def body(features, norm_gain, conv_weight, cotangent):
    frames, height, width, channels = features.shape
    inner = height * width
    cells = frames * inner
    depth, rows_of, cols_of = (lax.axis_size(axis) for axis in AXES)
    chips = rows_of // 2
    owned = channels // (rows_of * cols_of)
    half = channels // 2
    me_t, me_h, me_w = (lax.axis_index(axis) for axis in AXES)
    chip = me_h // 2
    where = jnp.stack([me_h % 2, me_w % 2, me_t % 2]).astype(jnp.int32)
    flat_x = features.reshape(cells, channels)
    slot = -(-(frames + 2) // 8) * 8
    framed_cot = cotangent.reshape(frames, inner, channels)
    gain = norm_gain.reshape(1, channels)
    product = 2 * cells * channels * channels
    size = 2 * cells * channels
    tall = height + CORNERS
    around = 2 * width + 2 * tall

    act, act_t, for_even, for_odd, kept = call(
        prepare_kernel,
        (
            shape_of(*features.shape),
            shape_of(channels, cells),
            shape_of(2, *features.shape[1:]),
            shape_of(2, *features.shape[1:]),
            shape_of(*features.shape),
        ),
        10 * cells * channels,
        3 * size,
        scalars=1,
        arrays=3,
        limit=12,
    )(where, features, gain, cotangent)
    met = [swap_pairs(for_even, "ta", 0), swap_pairs(for_odd, "ta", 1)]
    met = [array for array in met if array is not None]
    later, earlier, for_even, for_odd, lefts, rights = call(
        functools.partial(rows_kernel, len(met)),
        (
            shape_of(2, *features.shape[1:]),
            shape_of(2, *features.shape[1:]),
            shape_of(2, frames + 2, width, channels),
            shape_of(2, frames + 2, width, channels),
            shape_of(2, frames + 2, height, channels),
            shape_of(2, frames + 2, height, channels),
        ),
        0,
        2 * size,
        scalars=1,
        arrays=2 + len(met),
        limit=12,
    )(where, kept, act, *met)
    mine, send = call(
        functools.partial(own_kernel, chips),
        (
            shape_of(frames, inner, half),
            shape_of(cells // half * channels + cells, half),
        ),
        0,
        2 * size,
        scalars=1,
        arrays=2,
        left=1,
        limit=12,
    )(where, kept.reshape(framed_cot.shape), act_t, for_even)
    other = swap_core(send)
    rows = [swap_pairs(for_even, "ha", 0), swap_pairs(for_odd, "ha", 1)]
    rows = [array for array in rows if array is not None]
    mine, *by_swap = call(
        functools.partial(columns_kernel, len(rows), slot),
        (shape_of(frames, inner, half),)
        + (shape_of(2, (frames + 2) * height + 2 * slot, channels),) * min(2, cols_of - 1),
        0,
        size // 2,
        scalars=1,
        arrays=3 + len(rows),
        left=1,
    )(where, lefts, rights, *rows, mine, other)
    columns = [swap_pairs(array, "wa", odd) for odd, array in enumerate(by_swap)]
    later = later.reshape(2, inner, channels)
    cot_edges, act_edges, mine, send_more = call(
        functools.partial(bundle_kernel, chips, slot, (len(rows), len(columns))),
        (shape_of(frames + 2, around, channels),) * 2
        + (
            shape_of((frames + 2) * (inner + around), half),
            shape_of(2 * inner + (frames + 2) * around, half),
        ),
        0,
        size,
        scalars=1,
        arrays=2 + len(rows) + len(columns),
        limit=12,
    )(where, later, mine, *rows, *columns)
    other_more = swap_core(send_more)

    count = chips * cols_of
    moves = [(du, dw) for du in range(chips) for dw in range(cols_of)]
    places = jnp.stack(
        [((chip + du) % chips) * cols_of + (me_w + dw) % cols_of for du, dw in moves]
    ).astype(jnp.int32)
    offsets = [(i, j, k) for i in range(3) for j in range(3) for k in range(3)]
    terms = []
    for taps in (offsets[:FIRST_TAPS], offsets[FIRST_TAPS:]):
        reach = frames + taps[-1][0] - taps[0][0]
        spread = pltpu.VMEM((3, reach * (height + 2) * width, half), BF16)
        pieces = call(
            functools.partial(taps_kernel, height, width, taps),
            tuple(
                shape_of(len(taps), owned, channels, dtype=F32 if place == 0 else BF16)
                for place in range(count)
            ),
            len(taps) * product,
            4 * size,
            (pltpu.VMEM((len(taps), half, channels), F32), spread, spread),
            scalars=1,
            arrays=4,
            limit=16,
        )(places, act_t, mine, other, other_more)
        moved = [to_chip(piece, *move) for piece, move in zip(pieces[1:], moves[1:])]
        terms.append([pieces[0]] + moved)
        after = pieces[0]

    framed_act = act.reshape(frames, inner, channels)
    earlier = earlier.reshape(2, inner, channels)
    flat = (shape_of(cells, channels), shape_of(8, 128, dtype=F32))
    spread = pltpu.VMEM((3, (frames + 2) * (height + 2) * width, channels), BF16)
    touched = conv_weight.size * 2 + 4 * size
    grad_features, token_a = call(
        functools.partial(backward_kernel, height, width),
        flat,
        27 * product,
        touched,
        (spread,),
        arrays=6,
        left=1,
        limit=16,
    )(flat_x, gain, framed_cot, later, cot_edges, conv_weight, after)
    decoded, token_b = call(
        functools.partial(forward_kernel, height, width),
        flat,
        27 * product,
        touched,
        (spread,),
        arrays=5,
        left=1,
        limit=16,
    )(flat_x, earlier, framed_act, act_edges, conv_weight, after)

    part = -(-27 * owned // (16 * depth)) * 16
    owners = jnp.stack([partner(me_t, by, depth) for by in range(depth)]).astype(jnp.int32)
    own, *sends = call(
        functools.partial(parts_kernel, len(terms), count),
        tuple(
            shape_of(part, channels, dtype=F32 if by == 0 else BF16) for by in range(depth)
        ),
        0,
        2 * size,
        (pltpu.VMEM((depth, part, channels), F32),),
        scalars=1,
        arrays=count * len(terms),
        left=2,
    )(owners, *terms[0], *terms[1], token_a, token_b)
    for by, sent in enumerate(sends, 1):
        own = own + to_partner(sent, "ta", by).astype(F32)
    scale = float(cells * depth * rows_of * cols_of) ** (-0.5)
    own = (own * scale).astype(BF16)
    gathered = jnp.stack([own] + [to_partner(own, "ta", by) for by in range(1, depth)])
    if depth & (depth - 1) == 0:
        places = [me_t ^ rank for rank in range(depth)]
    else:
        places = [(me_t - rank) % depth for rank in range(depth)]
    gathered = jnp.concatenate(
        [lax.dynamic_index_in_dim(gathered, place, axis=0) for place in places]
    )
    grad_weight = gathered.reshape(depth * part, channels)[: 27 * owned]
    grad_weight = jnp.swapaxes(grad_weight.reshape(27, owned, channels), 1, 2).astype(F32)
    return (
        decoded.reshape(features.shape),
        grad_features.reshape(features.shape),
        grad_weight.reshape(3, 3, 3, channels, owned),
    )


def solution(mesh):
    placed = (P("ta", "ha", "wa", None), P(), P(), P("ta", "ha", "wa", None))
    return jax.shard_map(
        body,
        mesh=mesh,
        in_specs=placed,
        out_specs=(
            P("ta", "ha", "wa", None),
            P("ta", "ha", "wa", None),
            P(None, None, None, None, ("ha", "wa")),
        ),
        check_vma=False,
    )
```
